128 devices in a mesh: row: 8 (over z, x_hi), col: 16 (over x_lo, y, core).
Axes of the slice: x: 4 (x_hi: 2, x_lo: 2; x = x_hi * 2 + x_lo), y: 4, z: 4, core: 2. Of those that a mesh axis runs over, the one named last changes fastest.
Arguments:
- features: bfloat16 [131072, 256], P(('col', 'row')), may hold values from -6 to 6
- weight: bfloat16 [256, 256], replicated, may hold values from -0.375 to 0.375
- cotangent: bfloat16 [131072, 256], P(('row', 'col')), may hold values from -6 to 6
- tile_values: bfloat16 [8, 16, 384, 128, 128], P('row', 'col')
- tile_rows: int32 [8, 16, 384], P('row', 'col'), may hold values from 0 to 127, as said below
- tile_cols: int32 [8, 16, 384], P('row', 'col'), may hold values from 0 to 63
- tile_count: int32 [8, 16], P('row', 'col'), may hold values from 96 to 384, as said below
Outputs:
- activated: bfloat16 [131072, 256], P(('row', 'col'))
- weight_grad: float32 [256, 256], replicated
- feature_grad: bfloat16 [131072, 256], P(('col', 'row'))
The draws below stay inside these ranges and needn't reach their ends.
Inputs may be any that keep to these rules, and one draw needn't show every extreme that they name: `tile_rows`: on each device the slots name distinct (tile row, tile column) pairs. `tile_count`: some device uses all 384 slots in every draw.
All inputs are finite; a program needn't handle non-finite values.
Results may differ from the reference program's by a relative error of at most 0.025.
Values may be sent and summed in bfloat16 or wider, within the bound.
A program may use at most 192 MiB of HBM per device.

```python
import math
import jax
import jax.numpy as jnp
from jax import lax

F = 256
BLOCK = 128
NODES = 131072
RB = 128
CB = 64
TILES = 384
N_ROW = 8
N_COL = 16


def tile_pattern(key):
    keys = jax.random.split(key, N_ROW * N_COL)
    slots = RB * CB
    index = jnp.arange(slots, dtype=jnp.int32)
    near = jnp.abs(index // CB * CB - index % CB * RB) <= slots // 8

    def pick(single):
        score = jax.random.randint(single, (slots,), 0, 2 ** 14, dtype=jnp.int32)
        score = score + jnp.where(near, 2 ** 14, 0).astype(jnp.int32)
        distinct = score * slots + index
        unused, chosen = lax.top_k(distinct, TILES)
        return chosen.astype(jnp.int32)
    picked = jax.vmap(pick)(keys)
    return picked.reshape(N_ROW, N_COL, TILES)


def draw_tile_rows(key, part):
    shared = tile_pattern(key)
    return shared // CB


def draw_tile_cols(key, part):
    shared = tile_pattern(key)
    return shared % CB


def draw_tile_count(key, part):
    key = jax.random.fold_in(key, 3)
    divisor = jax.random.randint(key, (N_ROW * N_COL,), 1, 5, dtype=jnp.int32)
    counts = jnp.maximum(1, TILES // divisor)
    fullest = jax.random.randint(jax.random.fold_in(key, 5), (), 0, N_ROW * N_COL, dtype=jnp.int32)
    counts = jnp.where(jnp.arange(N_ROW * N_COL, dtype=jnp.int32) == fullest, TILES, counts)
    return counts.astype(jnp.int32).reshape(N_ROW, N_COL)


def draw_tile_values(key, part):
    key = jax.random.fold_in(key, 7)
    height = math.sqrt(3.0 * RB / (N_COL * TILES * BLOCK))
    shape = (N_ROW, N_COL, TILES, BLOCK, BLOCK)
    return (jax.random.uniform(key, shape, jnp.float32) * height).astype(jnp.bfloat16)


def levels(stream_key, extent, pieces, least, high):
    loudness, own = 1.0, jax.random.fold_in(stream_key, 6)
    for axis_at, blocks in pieces:
        draws = jnp.exp(jax.random.uniform(jax.random.fold_in(own, axis_at), (blocks,), jnp.float32, least / len(pieces), high / len(pieces)))
        loudness = loudness * jnp.repeat(draws, extent[axis_at] // blocks).reshape([-1 if axis == axis_at else 1 for axis in range(len(extent))])
    return loudness


def noise(key, shape, deviation, limit, shards=(), held_as=jnp.bfloat16):
    entries = deviation * jax.random.normal(key, shape, jnp.float32)
    if shards:
        entries = entries * levels(key, shape, shards, -0.22, 0.18)
    return jnp.clip(entries, -limit, limit).astype(held_as)


def setup_inputs(seed: int = 0) -> dict:
    key_of = jax.random.split(jax.random.key(seed), 8)
    return {
        "features": noise(key_of[0], (NODES, F), 1.0, 6.0, ((0, 128),)),
        "weight": noise(key_of[1], (F, F), F ** -0.5, 0.375),
        "cotangent": noise(key_of[2], (NODES, F), 1.0, 6.0, ((0, 128),)),
        "tile_values": draw_tile_values(jax.random.fold_in(key_of[7], 71), 0),
        "tile_rows": draw_tile_rows(jax.random.fold_in(key_of[7], 71), 0),
        "tile_cols": draw_tile_cols(jax.random.fold_in(key_of[7], 71), 0),
        "tile_count": draw_tile_count(jax.random.fold_in(key_of[7], 71), 0),
    }


def spread(values, dest, anchor, count, source, nblocks, flip):
    total = values.shape[0]
    group = math.gcd(total, 64)
    width = source.shape[-1]
    size = values.shape[1]

    def step(index, acc):
        start = (index * group).astype(jnp.int32)
        vals = lax.dynamic_slice_in_dim(values, start, group, 0).astype(jnp.float32)
        target = lax.dynamic_slice_in_dim(dest, start, group, 0)
        fetch = lax.dynamic_slice_in_dim(anchor, start, group, 0)
        picked = jnp.take(source, fetch, axis=0).astype(jnp.float32)
        if flip:
            prod = jnp.einsum('gba,gbf->gaf', vals, picked, precision=lax.Precision.HIGHEST)
        else:
            prod = jnp.einsum('gab,gbf->gaf', vals, picked, precision=lax.Precision.HIGHEST)
        live = start + jnp.arange(group, dtype=jnp.int32) < count
        target = jnp.where(live, target, jnp.int32(nblocks)).astype(jnp.int32)
        return acc + jax.ops.segment_sum(prod, target, num_segments=nblocks)
    start_acc = jnp.zeros((nblocks, size, width), jnp.float32)
    return lax.fori_loop(jnp.int32(0), jnp.int32(total // group), step, start_acc)

def reference(features, weight, cotangent, tile_values, tile_rows, tile_cols, tile_count):
    panels = features.reshape(N_COL, CB, BLOCK, F)

    def forward_row(row_index):

        def over_cols(acc, col_index):
            part = spread(tile_values[row_index, col_index], tile_rows[row_index, col_index], tile_cols[row_index, col_index], tile_count[row_index, col_index], panels[col_index], RB, False)
            return (acc + part.astype(jnp.bfloat16).astype(jnp.float32), None)
        total, unused = lax.scan(over_cols, jnp.zeros((RB, BLOCK, F), jnp.float32), jnp.arange(N_COL, dtype=jnp.int32))
        return total.astype(jnp.bfloat16)
    hidden = lax.map(forward_row, jnp.arange(N_ROW, dtype=jnp.int32)).reshape(NODES, F)
    pre = jnp.dot(hidden, weight, preferred_element_type=jnp.float32)
    activated = jax.nn.silu(pre).astype(jnp.bfloat16)
    sig = jax.nn.sigmoid(pre)
    delta = (cotangent.astype(jnp.float32) * sig * (1.0 + pre * (1.0 - sig))).astype(jnp.bfloat16)
    weight_grad = jnp.dot(hidden.T, delta, preferred_element_type=jnp.float32) / jnp.sqrt(jnp.float32(NODES))
    back = jnp.dot(delta, weight.T, preferred_element_type=jnp.float32).astype(jnp.bfloat16)
    back_rows = back.reshape(N_ROW, RB, BLOCK, F)

    def backward_col(col_index):

        def over_rows(acc, row_index):
            part = spread(tile_values[row_index, col_index], tile_cols[row_index, col_index], tile_rows[row_index, col_index], tile_count[row_index, col_index], back_rows[row_index], CB, True)
            return (acc + part.astype(jnp.bfloat16).astype(jnp.float32), None)
        total, unused = lax.scan(over_rows, jnp.zeros((CB, BLOCK, F), jnp.float32), jnp.arange(N_ROW, dtype=jnp.int32))
        return total.astype(jnp.bfloat16)
    feature_grad = lax.map(backward_col, jnp.arange(N_COL, dtype=jnp.int32)).reshape(NODES, F)
    return (activated, weight_grad, feature_grad)
```

```python
import functools

import jax
import jax.numpy as jnp
from jax import lax
from jax.experimental import pallas as pl
from jax.experimental.pallas import tpu as pltpu
from jax.sharding import PartitionSpec as P


def spread_kernel(flip, nblocks, group, unroll, count_ref, dest_ref, anchor_ref, v_ref, s_ref, o_ref, acc):
    step = pl.program_id(0)
    @pl.when(step == 0)
    def _():
        def z(i, _):
            acc[i] = jnp.zeros(acc.shape[1:], jnp.float32)
            return 0
        lax.fori_loop(0, nblocks, z, 0)
    count = count_ref[0]
    def sub(j, _):
        prods = []
        for u in range(unroll):
            t = j * unroll + u
            slot = step * group + t
            src = s_ref[anchor_ref[slot]]
            v = v_ref[t]
            if flip:
                p = lax.dot_general(v, src, (((0,), (0,)), ((), ())), preferred_element_type=jnp.float32)
            else:
                p = jnp.dot(v, src, preferred_element_type=jnp.float32)
            prods.append(jnp.where(slot < count, p, 0.0))
        for u in range(unroll):
            slot = step * group + j * unroll + u
            acc[dest_ref[slot]] += prods[u]
        return 0
    lax.fori_loop(0, group // unroll, sub, 0)
    @pl.when(step == pl.num_programs(0) - 1)
    def _():
        def w(i, _):
            o_ref[i] = acc[i].astype(jnp.bfloat16)
            return 0
        lax.fori_loop(0, nblocks, w, 0)

def spread(values, dest, anchor, count, source, nblocks, flip, group=32, unroll=8):
    total, size, _ = values.shape
    width = source.shape[-1]
    return pl.pallas_call(
        functools.partial(spread_kernel, flip, nblocks, group, unroll),
        grid_spec=pltpu.PrefetchScalarGridSpec(
            num_scalar_prefetch=3,
            grid=(total // group,),
            in_specs=[pl.BlockSpec((group, size, size), lambda i, *_: (i, 0, 0)),
                      pl.BlockSpec(source.shape, lambda i, *_: (0, 0, 0), pipeline_mode=pl.Buffered(1))],
            out_specs=pl.BlockSpec((nblocks, size, width), lambda i, *_: (0, 0, 0), pipeline_mode=pl.Buffered(1)),
            scratch_shapes=[pltpu.VMEM((nblocks, size, width), jnp.float32)],
        ),
        out_shape=jax.ShapeDtypeStruct((nblocks, size, width), jnp.bfloat16),
        compiler_params=pltpu.CompilerParams(vmem_limit_bytes=58 * 2**20),
    )(count, dest, anchor, values, source)

def dense_steps(hidden, weight, cotangent):
    pre = jnp.dot(hidden, weight, preferred_element_type=jnp.float32)
    activated = jax.nn.silu(pre).astype(jnp.bfloat16)
    sig = jax.nn.sigmoid(pre)
    delta = (cotangent.astype(jnp.float32) * sig * (1.0 + pre * (1.0 - sig))).astype(jnp.bfloat16)
    return (activated, delta)


def per_device(features, weight, cotangent, tile_values, tile_rows, tile_cols, tile_count):
    values = tile_values[0, 0]
    rows_idx = tile_rows[0, 0]
    cols_idx = tile_cols[0, 0]
    count = tile_count[0]
    size = values.shape[1]
    width = features.shape[1]
    node_dev = features.shape[0]
    n_row = lax.axis_size("row")
    n_col = lax.axis_size("col")
    row_blocks = node_dev * n_col // size
    col_blocks = node_dev * n_row // size
    panel = lax.all_gather(features, "row", axis=0, tiled=True).reshape(col_blocks, size, width)
    part = spread(values, rows_idx, cols_idx, count, panel, row_blocks, False).reshape(
        row_blocks * size, width
    )
    part = part.astype(jnp.bfloat16)
    hidden = (
        lax.psum_scatter(part, "col", scatter_dimension=0, tiled=True)
        .astype(jnp.float32)
        .astype(jnp.bfloat16)
    )
    activated, delta = dense_steps(hidden, weight, cotangent)
    back = jnp.dot(delta, weight.T, preferred_element_type=jnp.float32).astype(jnp.bfloat16)
    back_block = lax.all_gather(back, "col", axis=0, tiled=True)
    grad_terms = jnp.einsum("nf,ng->fg", hidden, delta, preferred_element_type=jnp.float32)
    total_nodes = node_dev * n_row * n_col
    weight_grad = lax.psum(grad_terms, ("row", "col")) / jnp.sqrt(jnp.float32(total_nodes))
    source = back_block.reshape(row_blocks, size, width)
    tpart = spread(values, cols_idx, rows_idx, count, source, col_blocks, True).reshape(
        col_blocks * size, width
    )
    tpart = tpart.astype(jnp.bfloat16)
    feature_grad = (
        lax.psum_scatter(tpart, "row", scatter_dimension=0, tiled=True)
        .astype(jnp.float32)
        .astype(jnp.bfloat16)
    )
    return (activated, weight_grad, feature_grad)


def solution(mesh):
    return jax.shard_map(
        per_device,
        mesh=mesh,
        in_specs=(
            P(("col", "row"), None),
            P(),
            P(("row", "col"), None),
            P("row", "col", None, None, None),
            P("row", "col", None),
            P("row", "col", None),
            P("row", "col"),
        ),
        out_specs=(P(("row", "col"), None), P(), P(("col", "row"), None)),
        check_vma=False,
    )
```

```python
import functools

import jax
import jax.numpy as jnp
from jax import lax
from jax.experimental import pallas as pl
from jax.experimental.pallas import tpu as pltpu
from jax.sharding import PartitionSpec as P

BF16 = jnp.bfloat16
F32 = jnp.float32
STEP = 32


def place():
    r = lax.axis_index("row")
    c = lax.axis_index("col")
    return r // 2, r % 2, c // 8, (c // 2) % 4, c % 2


def row_device(z, xh):
    return (z * 2 + xh, lax.axis_index("col"))


def col_device(xl, y, k):
    return (lax.axis_index("row"), xl * 8 + y * 2 + k)


def greet(peers):
    barrier = pltpu.get_barrier_semaphore()
    for peer in peers:
        pl.semaphore_signal(barrier, inc=1, device_id=peer, device_id_type=pl.DeviceIdType.MESH)
    pl.semaphore_wait(barrier, len(peers))


class Mover:
    def __init__(self, send_sem, recv_sem, local_sem):
        self.send_sem, self.recv_sem, self.local_sem = send_sem, recv_sem, local_sem
        self.sent = []
        self.kept = 0

    def remote(self, src, dst, device):
        at = len(self.sent)
        copy = pltpu.make_async_remote_copy(
            src_ref=src,
            dst_ref=dst,
            send_sem=self.send_sem.at[at],
            recv_sem=self.recv_sem.at[at],
            device_id=device,
            device_id_type=pl.DeviceIdType.MESH,
        )
        copy.start()
        self.sent.append(copy)
        return copy

    def local(self, src, dst):
        copy = pltpu.make_async_copy(src, dst, self.local_sem.at[self.kept])
        copy.start()
        self.kept += 1
        return copy

    def drain(self):
        for copy in self.sent:
            copy.wait_send()


def add_rows(dst, terms, rows):
    def body(i, carry):
        at = pl.ds(pl.multiple_of(i * STEP, STEP), STEP)
        total = terms[0][at, :].astype(F32)
        for term in terms[1:]:
            total = total + term[at, :].astype(F32)
        dst[at, :] = total.astype(dst.dtype)
        return carry

    lax.fori_loop(0, rows // STEP, body, 0)


def split(rows):
    first = rows * 7 // 16 // (2 * STEP) * (2 * STEP)
    rest = rows - first
    return {
        "A": (0, first),
        "A0": (0, first // 2),
        "A1": (first // 2, first // 2),
        "B": (first, rest),
        "B0": (first, rest // 2),
        "B1": (first + rest // 2, rest // 2),
    }


def gather_pieces(mv, own, out, slot, rows, ring, pair, p, q, arrived):
    parts = split(rows)
    plus, minus = ring
    at = lambda d: (p + d) % 4

    def reg(d, side, name):
        start, size = parts[name]
        which = q if side == 0 else 1 - q
        return out.at[slot(at(d), which), pl.ds(start, size)]

    def mine(name):
        start, size = parts[name]
        return own.at[pl.ds(start, size)]

    def fwd(d, side, name, device):
        return mv.remote(reg(d, side, name), reg(d, side, name), device)

    pair_b = mv.remote(mine("B"), reg(0, 0, "B"), pair)
    a_plus = mv.remote(mine("A"), reg(0, 0, "A"), plus)
    a_minus = mv.remote(mine("A"), reg(0, 0, "A"), minus)
    b_plus = mv.remote(mine("B"), reg(0, 0, "B"), plus)
    b_minus = mv.remote(mine("B"), reg(0, 0, "B"), minus)
    pair_a = [mv.remote(mine("A"), reg(0, 0, "A"), pair)]
    a_plus.wait_recv()
    ra_plus = fwd(3, 0, "A0", plus)
    pair_a.append(fwd(3, 0, "A", pair))
    a_minus.wait_recv()
    ra_minus = fwd(1, 0, "A1", minus)
    pair_a.append(fwd(1, 0, "A", pair))
    arrived(reg(3, 0, "A"))
    arrived(reg(1, 0, "A"))
    pair_b.wait_recv()
    pb_plus = fwd(0, 1, "B", plus)
    pb_minus = fwd(0, 1, "B", minus)
    arrived(reg(0, 1, "B"))
    b_plus.wait_recv()
    rb_plus = fwd(3, 0, "B0", plus)
    b_minus.wait_recv()
    rb_minus = fwd(1, 0, "B1", minus)
    arrived(reg(3, 0, "B"))
    arrived(reg(1, 0, "B"))
    ra_plus.wait_recv()
    pair_a.append(fwd(2, 0, "A0", pair))
    ra_minus.wait_recv()
    pair_a.append(fwd(2, 0, "A1", pair))
    arrived(reg(2, 0, "A"))
    pb_plus.wait_recv()
    rpb_plus = fwd(3, 1, "B0", plus)
    pb_minus.wait_recv()
    rpb_minus = fwd(1, 1, "B1", minus)
    arrived(reg(3, 1, "B"))
    arrived(reg(1, 1, "B"))
    rb_plus.wait_recv()
    rb_minus.wait_recv()
    arrived(reg(2, 0, "B"))
    for d, copy in zip((0, 3, 1), pair_a):
        copy.wait_recv()
        arrived(reg(d, 1, "A"))
    pair_a[3].wait_recv()
    pair_a[4].wait_recv()
    arrived(reg(2, 1, "A"))
    rpb_plus.wait_recv()
    rpb_minus.wait_recv()
    arrived(reg(2, 1, "B"))


def scatter_scratch(rows):
    parts = split(rows)
    first, rest = parts["A"][1], parts["B"][1]
    width = 256
    return [
        pltpu.VMEM((4, first, width), BF16),
        pltpu.VMEM((2, 2, rest // 2, width), BF16),
        pltpu.VMEM((2, 2, rest, width), BF16),
        pltpu.VMEM((2, first // 2, width), BF16),
        pltpu.VMEM((2, first, width), BF16),
        pltpu.VMEM((rest, width), BF16),
    ]


def scatter_pieces(mv, held, slot, bufs, out, rows, ring, pair, p, q, ready):
    parts = split(rows)
    plus, minus = ring
    ra, rb1, rb2, ra1, ra2, rp = bufs
    nb, na = parts["B"][1], parts["A"][1]
    at = lambda d: (p + d) % 4

    def reg(d, side, name):
        start, size = parts[name]
        which = q if side == 0 else 1 - q
        return held.at[slot(at(d), which), pl.ds(start, size)]

    def b_half(ref, h):
        return ref.at[pl.ds(h * (nb // 2), nb // 2)]

    def a_half(ref, h):
        return ref.at[pl.ds(h * (na // 2), na // 2)]

    def ring_b(side, d):
        pass

    got_b1 = {}
    got_b2 = {}
    got_a = {}
    for side in (1, 0):
        ready(at(2), q if side == 0 else 1 - q)
        got_b1[0, side] = mv.remote(reg(2, side, "B0"), rb1.at[0, side], plus)
        got_b1[1, side] = mv.remote(reg(2, side, "B1"), rb1.at[1, side], minus)
        if side == 1:
            got_a[2] = mv.remote(reg(2, 1, "A"), ra.at[2], pair)
    for side in (1, 0):
        ready(at(1), q if side == 0 else 1 - q)
        got_b2[0, side, 1] = mv.remote(reg(1, side, "B1"), b_half(rb2.at[0, side], 1), plus)
        if side == 1:
            got_a[1] = mv.remote(reg(1, 1, "A"), ra.at[1], pair)
        ready(at(3), q if side == 0 else 1 - q)
        got_b2[1, side, 0] = mv.remote(reg(3, side, "B0"), b_half(rb2.at[1, side], 0), minus)
        if side == 1:
            got_a[3] = mv.remote(reg(3, 1, "A"), ra.at[3], pair)
    ready(at(0), 1 - q)
    got_a[0] = mv.remote(reg(0, 1, "A"), ra.at[0], pair)
    ready(at(0), q)
    for side in (1, 0):
        got_b1[0, side].wait_recv()
        add_rows(reg(1, side, "B0"), [reg(1, side, "B0"), rb1.at[0, side]], nb // 2)
        got_b2[0, side, 0] = mv.remote(reg(1, side, "B0"), b_half(rb2.at[0, side], 0), plus)
        got_b1[1, side].wait_recv()
        add_rows(reg(3, side, "B1"), [reg(3, side, "B1"), rb1.at[1, side]], nb // 2)
        got_b2[1, side, 1] = mv.remote(reg(3, side, "B1"), b_half(rb2.at[1, side], 1), minus)
    got_a[2].wait_recv()
    add_rows(reg(2, 0, "A"), [reg(2, 0, "A"), ra.at[2]], na)
    got_a1 = [mv.remote(reg(2, 0, "A0"), ra1.at[0], plus), mv.remote(reg(2, 0, "A1"), ra1.at[1], minus)]
    got_a[1].wait_recv()
    add_rows(reg(1, 0, "A"), [reg(1, 0, "A"), ra.at[1]], na)
    got_a2 = {}
    got_a2[0, 1] = mv.remote(reg(1, 0, "A1"), a_half(ra2.at[0], 1), plus)
    got_a[3].wait_recv()
    add_rows(reg(3, 0, "A"), [reg(3, 0, "A"), ra.at[3]], na)
    got_a2[1, 0] = mv.remote(reg(3, 0, "A0"), a_half(ra2.at[1], 0), minus)
    for way in (0, 1):
        for h in (0, 1):
            got_b2[way, 1, h].wait_recv()
    add_rows(reg(0, 1, "B"), [reg(0, 1, "B"), rb2.at[0, 1], rb2.at[1, 1]], nb)
    got_p = mv.remote(reg(0, 1, "B"), rp, pair)
    got_a1[0].wait_recv()
    add_rows(reg(1, 0, "A0"), [reg(1, 0, "A0"), ra1.at[0]], na // 2)
    got_a2[0, 0] = mv.remote(reg(1, 0, "A0"), a_half(ra2.at[0], 0), plus)
    got_a1[1].wait_recv()
    add_rows(reg(3, 0, "A1"), [reg(3, 0, "A1"), ra1.at[1]], na // 2)
    got_a2[1, 1] = mv.remote(reg(3, 0, "A1"), a_half(ra2.at[1], 1), minus)
    for way in (0, 1):
        for h in (0, 1):
            got_b2[way, 0, h].wait_recv()
    got_p.wait_recv()
    add_rows(out.at[pl.ds(na, nb)], [reg(0, 0, "B"), rb2.at[0, 0], rb2.at[1, 0], rp], nb)
    got_a[0].wait_recv()
    for way in (0, 1):
        for h in (0, 1):
            got_a2[way, h].wait_recv()
    add_rows(out.at[pl.ds(0, na)], [reg(0, 0, "A"), ra.at[0], ra2.at[0], ra2.at[1]], na)


COMM = dict(has_side_effects=True, vmem_limit_bytes=48 * 2**20)
ANY = pl.BlockSpec(memory_space=pl.ANY)
VMEM = pl.BlockSpec(memory_space=pltpu.VMEM)


def row_links():
    z, xh, xl, y, k = place()
    ring = (row_device((z + 1) % 4, xh), row_device((z + 3) % 4, xh))
    return ring, row_device(z, 1 - xh), z, xh


def col_links():
    z, xh, xl, y, k = place()
    ring = (col_device(xl, (y + 1) % 4, k), col_device(xl, (y + 3) % 4, k))
    return ring, col_device(1 - xl, y, k), y, xl


def gather_row_kernel(x_ref, out_ref, send_sem, recv_sem, local_sem):
    ring, pair, p, q = row_links()
    greet([*ring, pair])
    mv = Mover(send_sem, recv_sem, local_sem)
    slot = lambda z, xh: z * 2 + xh
    keep = mv.local(x_ref, out_ref.at[slot(p, q)])
    gather_pieces(mv, x_ref, out_ref, slot, x_ref.shape[0], ring, pair, p, q, lambda ref: None)
    keep.wait()
    mv.drain()


def gather_row(x):
    rows, width = x.shape
    return pl.pallas_call(
        gather_row_kernel,
        out_shape=jax.ShapeDtypeStruct((8, rows, width), BF16),
        in_specs=[ANY],
        out_specs=ANY,
        scratch_shapes=[pltpu.SemaphoreType.DMA((20,)), pltpu.SemaphoreType.DMA((20,)), pltpu.SemaphoreType.DMA((1,))],
        compiler_params=pltpu.CompilerParams(collective_id=1, **COMM),
    )(x)


def middle_kernel(part_ref, w_ref, cot_ref, act_ref, gt_ref, back_ref, held, met, hidden, back, delta, *rest):
    bufs, (send_sem, recv_sem, local_sem) = rest[:6], rest[6:]
    z, xh, xl, y, k = place()
    ring, pair, p, q = col_links()
    twin = col_device(xl, y, 1 - k)
    greet([*ring, pair, twin])
    mv = Mover(send_sem, recv_sem, local_sem)
    rows = hidden.shape[0]
    slot8 = lambda p_, q_: q_ * 4 + p_
    slot16 = lambda p_, q_, k_: (q_ * 4 + p_) * 2 + k_
    crossing, loading = [], []
    order = [(2, 1), (2, 0), (1, 1), (3, 1), (1, 0), (3, 0), (0, 1), (0, 0)]
    for d, side in order:
        p_ = (p + d) % 4
        q_ = q if side == 0 else 1 - q
        crossing.append(mv.remote(part_ref.at[slot16(p_, q_, 1 - k)], met.at[slot8(p_, q_)], twin))
        loading.append(mv.local(part_ref.at[slot16(p_, q_, k)], held.at[slot8(p_, q_)]))
    step = [0]

    def ready(p_, q_):
        i = step[0]
        step[0] += 1
        crossing[i].wait_recv()
        loading[i].wait()
        ref = held.at[slot8(p_, q_)]
        add_rows(ref, [ref, met.at[slot8(p_, q_)]], rows)

    scatter_pieces(mv, held, slot8, bufs, hidden, rows, ring, pair, p, q, ready)
    chunk = 128

    def dense(i, carry):
        at = pl.ds(pl.multiple_of(i * chunk, chunk), chunk)
        pre = jnp.dot(hidden[at, :], w_ref[...], preferred_element_type=F32)
        sig = 1.0 / (1.0 + jnp.exp(-pre))
        act_ref[at, :] = (pre * sig).astype(BF16)
        d = (cot_ref[at, :].astype(F32) * sig * (1.0 + pre * (1.0 - sig))).astype(BF16)
        delta[at, :] = d
        back[at, :] = lax.dot_general(
            d, w_ref[...], (((1,), (1,)), ((), ())), preferred_element_type=F32
        ).astype(BF16)
        return carry

    lax.fori_loop(0, rows // chunk, dense, 0)
    keep = mv.local(back, back_ref.at[slot16(p, q, k)])
    shares = [mv.remote(back, back_ref.at[slot16(p, q, k)], twin)]
    terms = []

    def arrived(ref):
        if not terms:
            terms.append(1)
            gt_ref[...] = lax.dot_general(
                hidden[...], delta[...], (((0,), (0,)), ((), ())), preferred_element_type=F32
            )
        shares.append(mv.remote(ref, ref, twin))

    gather_pieces(mv, back, back_ref, lambda p_, q_: slot16(p_, q_, k), rows, ring, pair, p, q, arrived)
    for share in shares:
        share.wait_recv()
    keep.wait()
    mv.drain()


def middle(part, weight, cotangent):
    rows, width = cotangent.shape
    return pl.pallas_call(
        middle_kernel,
        out_shape=(
            jax.ShapeDtypeStruct((rows, width), BF16),
            jax.ShapeDtypeStruct((width, width), F32),
            jax.ShapeDtypeStruct((16, rows, width), BF16),
        ),
        in_specs=[ANY, VMEM, VMEM],
        out_specs=(VMEM, VMEM, ANY),
        scratch_shapes=[
            pltpu.VMEM((8, rows, width), BF16),
            pltpu.VMEM((8, rows, width), BF16),
            pltpu.VMEM((rows, width), BF16),
            pltpu.VMEM((rows, width), BF16),
            pltpu.VMEM((rows, width), BF16),
            *scatter_scratch(rows),
            pltpu.SemaphoreType.DMA((80,)),
            pltpu.SemaphoreType.DMA((80,)),
            pltpu.SemaphoreType.DMA((12,)),
        ],
        compiler_params=pltpu.CompilerParams(collective_id=2, **COMM),
    )(part.reshape(16, rows, width), weight, cotangent)


def finish_kernel(nodes, tpart_ref, gt_ref, fg_ref, wg_ref, held, wr1, ws1, wr2, *rest):
    bufs, (send_sem, recv_sem, local_sem) = rest[:6], rest[6:]
    r0 = lax.axis_index("row")
    c0 = lax.axis_index("col")
    ring, pair, p, q = row_links()
    row_peers = [((r0 + j) % 8, c0) for j in range(1, 8)]
    col_peers = [(r0, (c0 + j) % 16) for j in range(1, 16)]
    greet(row_peers + col_peers)
    mv = Mover(send_sem, recv_sem, local_sem)
    rows = fg_ref.shape[0]
    slot = lambda z, xh: z * 2 + xh
    order = [(2, 1), (2, 0), (1, 1), (3, 1), (1, 0), (3, 0), (0, 1), (0, 0)]
    loading = []
    for d, side in order:
        s = slot((p + d) % 4, q if side == 0 else 1 - q)
        loading.append(mv.local(tpart_ref.at[s], held.at[s]))
    first = []
    for j in range(1, 16):
        at = pl.ds(pl.multiple_of((c0 + j) % 16 * 16, 16), 16)
        first.append(mv.remote(gt_ref.at[at], wr1.at[j], col_peers[j - 1]))
    step = [0]

    def ready(p_, q_):
        loading[step[0]].wait()
        step[0] += 1

    scatter_pieces(mv, held, slot, bufs, fg_ref, rows, ring, pair, p, q, ready)

    mine = pl.ds(pl.multiple_of(c0 * 16, 16), 16)
    for copy in first:
        copy.wait_recv()
    total = gt_ref[mine, :]
    for j in range(1, 16):
        total = total + wr1[j]
    wr2[r0] = total
    second = [mv.remote(wr2.at[r0], wr2.at[r0], peer) for peer in row_peers]
    for copy in second:
        copy.wait_recv()
    total = wr2[0]
    for j in range(1, 8):
        total = total + wr2[j]
    wg_ref[mine, :] = total / jnp.sqrt(F32(nodes))
    third = [mv.remote(wg_ref.at[mine], wg_ref.at[mine], peer) for peer in col_peers]
    for copy in third:
        copy.wait_recv()
    mv.drain()


def finish(tpart, grad_terms, rows, nodes):
    width = tpart.shape[-1]
    return pl.pallas_call(
        functools.partial(finish_kernel, nodes),
        out_shape=(
            jax.ShapeDtypeStruct((rows, width), BF16),
            jax.ShapeDtypeStruct((width, width), F32),
        ),
        in_specs=[ANY, VMEM],
        out_specs=(VMEM, VMEM),
        scratch_shapes=[
            pltpu.VMEM((8, rows, width), BF16),
            pltpu.VMEM((16, 16, width), F32),
            pltpu.VMEM((16, width), F32),
            pltpu.VMEM((8, 16, width), F32),
            *scatter_scratch(rows),
            pltpu.SemaphoreType.DMA((80,)),
            pltpu.SemaphoreType.DMA((80,)),
            pltpu.SemaphoreType.DMA((8,)),
        ],
        compiler_params=pltpu.CompilerParams(collective_id=3, **COMM),
    )(tpart.reshape(8, rows, width), grad_terms)


def spread_kernel(flip, nblocks, group, unroll, count_ref, dest_ref, anchor_ref, v_ref, s_ref, o_ref, acc):
    step = pl.program_id(0)
    @pl.when(step == 0)
    def _():
        def z(i, _):
            acc[i] = jnp.zeros(acc.shape[1:], jnp.float32)
            return 0
        lax.fori_loop(0, nblocks, z, 0)
    count = count_ref[0]
    def sub(j, _):
        prods = []
        for u in range(unroll):
            t = j * unroll + u
            slot = step * group + t
            src = s_ref[anchor_ref[slot]]
            v = v_ref[t]
            if flip:
                p = lax.dot_general(v, src, (((0,), (0,)), ((), ())), preferred_element_type=jnp.float32)
            else:
                p = jnp.dot(v, src, preferred_element_type=jnp.float32)
            prods.append(jnp.where(slot < count, p, 0.0))
        for u in range(unroll):
            slot = step * group + j * unroll + u
            acc[dest_ref[slot]] += prods[u]
        return 0
    lax.fori_loop(0, group // unroll, sub, 0)
    @pl.when(step == pl.num_programs(0) - 1)
    def _():
        def w(i, _):
            o_ref[i] = acc[i].astype(jnp.bfloat16)
            return 0
        lax.fori_loop(0, nblocks, w, 0)

def spread(values, dest, anchor, count, source, nblocks, flip, group=32, unroll=8):
    total, size, _ = values.shape
    width = source.shape[-1]
    return pl.pallas_call(
        functools.partial(spread_kernel, flip, nblocks, group, unroll),
        grid_spec=pltpu.PrefetchScalarGridSpec(
            num_scalar_prefetch=3,
            grid=(total // group,),
            in_specs=[pl.BlockSpec((group, size, size), lambda i, *_: (i, 0, 0)),
                      pl.BlockSpec(source.shape, lambda i, *_: (0, 0, 0), pipeline_mode=pl.Buffered(1))],
            out_specs=pl.BlockSpec((nblocks, size, width), lambda i, *_: (0, 0, 0), pipeline_mode=pl.Buffered(1)),
            scratch_shapes=[pltpu.VMEM((nblocks, size, width), jnp.float32)],
        ),
        out_shape=jax.ShapeDtypeStruct((nblocks, size, width), jnp.bfloat16),
        compiler_params=pltpu.CompilerParams(vmem_limit_bytes=58 * 2**20),
    )(count, dest, anchor, values, source)


def per_device(features, weight, cotangent, tile_values, tile_rows, tile_cols, tile_count):
    values = tile_values[0, 0]
    rows_idx = tile_rows[0, 0]
    cols_idx = tile_cols[0, 0]
    count = tile_count[0]
    size = values.shape[1]
    rows, width = features.shape
    n_row = lax.axis_size("row")
    n_col = lax.axis_size("col")
    row_blocks = rows * n_col // size
    col_blocks = rows * n_row // size
    panel = gather_row(features).reshape(col_blocks, size, width)
    part = spread(values, rows_idx, cols_idx, count, panel, row_blocks, False)
    activated, grad_terms, back_block = middle(part, weight, cotangent)
    source = back_block.reshape(row_blocks, size, width)
    tpart = spread(values, cols_idx, rows_idx, count, source, col_blocks, True)
    feature_grad, weight_grad = finish(tpart, grad_terms, rows, rows * n_row * n_col)
    return (activated, weight_grad, feature_grad)


def solution(mesh):
    return jax.shard_map(
        per_device,
        mesh=mesh,
        in_specs=(
            P(("col", "row"), None),
            P(),
            P(("row", "col"), None),
            P("row", "col", None, None, None),
            P("row", "col", None),
            P("row", "col", None),
            P("row", "col"),
        ),
        out_specs=(P(("row", "col"), None), P(), P(("col", "row"), None)),
        check_vma=False,
    )
```

```python
import functools

import jax
import jax.numpy as jnp
from jax import lax
from jax.experimental import pallas as pl
from jax.experimental.pallas import tpu as pltpu
from jax.sharding import PartitionSpec as P

BF16 = jnp.bfloat16
F32 = jnp.float32
UNROLL = 24
SIDE = 128


def place():
    r = lax.axis_index("row")
    c = lax.axis_index("col")
    return r // 2, r % 2, c // 8, (c // 2) % 4, c % 2


def row_device(z, xh):
    return (z * 2 + xh, lax.axis_index("col"))


def col_device(xl, y, k):
    return (lax.axis_index("row"), xl * 8 + y * 2 + k)


def greet(peers):
    barrier = pltpu.get_barrier_semaphore()
    for peer in peers:
        pl.semaphore_signal(barrier, inc=1, device_id=peer, device_id_type=pl.DeviceIdType.MESH)
    pl.semaphore_wait(barrier, len(peers))


class Mover:
    def __init__(self, send_sem, recv_sem, local_sem):
        self.send_sem, self.recv_sem, self.local_sem = send_sem, recv_sem, local_sem
        self.started = 0
        self.kept = 0
        self.pending = []

    def remote(self, src, dst, device):
        at = self.started
        self.started += 1
        copy = pltpu.make_async_remote_copy(
            src_ref=src,
            dst_ref=dst,
            send_sem=self.send_sem.at[at],
            recv_sem=self.recv_sem.at[at],
            device_id=device,
            device_id_type=pl.DeviceIdType.MESH,
        )
        copy.start()
        self.pending.append(copy)
        return copy

    def local(self, src, dst):
        copy = pltpu.make_async_copy(src, dst, self.local_sem.at[self.kept])
        copy.start()
        self.kept += 1
        return copy

    def drain(self):
        for copy in self.take():
            copy.wait_send()

    def take(self):
        copies, self.pending = self.pending, []
        return copies


def add_blocks(dst, terms, blocks):
    def body(i, carry):
        total = terms[0][i].astype(F32)
        for term in terms[1:]:
            total = total + term[i].astype(F32)
        dst[i] = total.astype(dst.dtype)
        return carry

    lax.fori_loop(0, blocks, body, 0)


def split(blocks):
    first = blocks // 4
    rest = blocks - first
    return {
        "A": (0, first),
        "A0": (0, first // 2),
        "A1": (first // 2, first // 2),
        "B": (first, rest),
        "B0": (first, rest // 2),
        "B1": (first + rest // 2, rest // 2),
    }


class Links:
    def __init__(self, ring, pair, p, q, slot, blocks):
        self.ring, self.pair, self.p, self.q, self.slot, self.blocks = ring, pair, p, q, slot, blocks

    def piece(self, d, side):
        return self.slot((self.p + d) % 4, self.q if side == 0 else 1 - self.q)

    def part(self, ref, d, side, name=None):
        start, size = split(self.blocks)[name] if name else (0, self.blocks)
        return ref.at[pl.ds(self.piece(d, side) * self.blocks + start, size)]


def gather_steps(mv, links, out, arrived):
    plus, minus = links.ring
    pair = links.pair
    reg = functools.partial(links.part, out)

    def go(d, side, name, device):
        return mv.remote(reg(d, side, name), reg(d, side, name), device)

    pair_b = go(0, 0, "B", pair)
    a_plus = go(0, 0, "A", plus)
    a_minus = go(0, 0, "A", minus)
    b_plus = go(0, 0, "B", plus)
    b_minus = go(0, 0, "B", minus)
    pair_a = [go(0, 0, "A", pair)]
    yield
    a_plus.wait_recv()
    ra_plus = go(3, 0, "A0", plus)
    pair_a.append(go(3, 0, "A", pair))
    a_minus.wait_recv()
    ra_minus = go(1, 0, "A1", minus)
    pair_a.append(go(1, 0, "A", pair))
    arrived(reg(3, 0, "A"))
    arrived(reg(1, 0, "A"))
    yield
    pair_b.wait_recv()
    pb_plus = go(0, 1, "B", plus)
    pb_minus = go(0, 1, "B", minus)
    arrived(reg(0, 1, "B"))
    yield
    b_plus.wait_recv()
    rb_plus = go(3, 0, "B0", plus)
    b_minus.wait_recv()
    rb_minus = go(1, 0, "B1", minus)
    arrived(reg(3, 0, "B"))
    arrived(reg(1, 0, "B"))
    yield
    ra_plus.wait_recv()
    pair_a.append(go(2, 0, "A0", pair))
    ra_minus.wait_recv()
    pair_a.append(go(2, 0, "A1", pair))
    arrived(reg(2, 0, "A"))
    yield
    pb_plus.wait_recv()
    rpb_plus = go(3, 1, "B0", plus)
    pb_minus.wait_recv()
    rpb_minus = go(1, 1, "B1", minus)
    arrived(reg(3, 1, "B"))
    arrived(reg(1, 1, "B"))
    yield
    rb_plus.wait_recv()
    rb_minus.wait_recv()
    arrived(reg(2, 0, "B"))
    for d, copy in zip((0, 3, 1), pair_a):
        yield
        copy.wait_recv()
        arrived(reg(d, 1, "A"))
    yield
    pair_a[3].wait_recv()
    pair_a[4].wait_recv()
    arrived(reg(2, 1, "A"))
    yield
    rpb_plus.wait_recv()
    rpb_minus.wait_recv()
    arrived(reg(2, 1, "B"))


def scatter_scratch(blocks):
    parts = split(blocks)
    first, rest = parts["A"][1], parts["B"][1]
    return [
        pltpu.VMEM((4, first, SIDE, SIDE), BF16),
        pltpu.VMEM((2, 2, rest // 2, SIDE, SIDE), BF16),
        pltpu.VMEM((2, 2, rest, SIDE, SIDE), BF16),
        pltpu.VMEM((2, first // 2, SIDE, SIDE), BF16),
        pltpu.VMEM((2, first, SIDE, SIDE), BF16),
        pltpu.VMEM((rest, SIDE, SIDE), BF16),
    ]


ORDER = ((2, 1), (2, 0), (1, 1), (3, 1), (1, 0), (3, 0), (0, 1), (0, 0))


def scatter_steps(mv, links, held, bufs, out, ready):
    parts = split(links.blocks)
    plus, minus = links.ring
    pair = links.pair
    ra, rb1, rb2, ra1, ra2, rp = bufs
    nb, na = parts["B"][1], parts["A"][1]
    reg = functools.partial(links.part, held)
    b_half = lambda ref, h: ref.at[pl.ds(h * (nb // 2), nb // 2)]
    a_half = lambda ref, h: ref.at[pl.ds(h * (na // 2), na // 2)]
    got_b1, got_b2, got_a, got_a2 = {}, {}, {}, {}
    for d, side in ORDER:
        yield
        ready(d, side)
        if d == 2:
            got_b1[0, side] = mv.remote(reg(2, side, "B0"), rb1.at[0, side], plus)
            got_b1[1, side] = mv.remote(reg(2, side, "B1"), rb1.at[1, side], minus)
        elif d == 1:
            got_b2[0, side, 1] = mv.remote(reg(1, side, "B1"), b_half(rb2.at[0, side], 1), plus)
        elif d == 3:
            got_b2[1, side, 0] = mv.remote(reg(3, side, "B0"), b_half(rb2.at[1, side], 0), minus)
        if side == 1:
            got_a[d] = mv.remote(reg(d, 1, "A"), ra.at[d], pair)
    for side in (1, 0):
        yield
        got_b1[0, side].wait_recv()
        add_blocks(reg(1, side, "B0"), [reg(1, side, "B0"), rb1.at[0, side]], nb // 2)
        got_b2[0, side, 0] = mv.remote(reg(1, side, "B0"), b_half(rb2.at[0, side], 0), plus)
        got_b1[1, side].wait_recv()
        add_blocks(reg(3, side, "B1"), [reg(3, side, "B1"), rb1.at[1, side]], nb // 2)
        got_b2[1, side, 1] = mv.remote(reg(3, side, "B1"), b_half(rb2.at[1, side], 1), minus)
    yield
    got_a[2].wait_recv()
    add_blocks(reg(2, 0, "A"), [reg(2, 0, "A"), ra.at[2]], na)
    got_a1 = [
        mv.remote(reg(2, 0, "A0"), ra1.at[0], plus),
        mv.remote(reg(2, 0, "A1"), ra1.at[1], minus),
    ]
    yield
    got_a[1].wait_recv()
    add_blocks(reg(1, 0, "A"), [reg(1, 0, "A"), ra.at[1]], na)
    got_a2[0, 1] = mv.remote(reg(1, 0, "A1"), a_half(ra2.at[0], 1), plus)
    got_a[3].wait_recv()
    add_blocks(reg(3, 0, "A"), [reg(3, 0, "A"), ra.at[3]], na)
    got_a2[1, 0] = mv.remote(reg(3, 0, "A0"), a_half(ra2.at[1], 0), minus)
    yield
    for way in (0, 1):
        for h in (0, 1):
            got_b2[way, 1, h].wait_recv()
    add_blocks(reg(0, 1, "B"), [reg(0, 1, "B"), rb2.at[0, 1], rb2.at[1, 1]], nb)
    got_p = mv.remote(reg(0, 1, "B"), rp, pair)
    yield
    got_a1[0].wait_recv()
    add_blocks(reg(1, 0, "A0"), [reg(1, 0, "A0"), ra1.at[0]], na // 2)
    got_a2[0, 0] = mv.remote(reg(1, 0, "A0"), a_half(ra2.at[0], 0), plus)
    got_a1[1].wait_recv()
    add_blocks(reg(3, 0, "A1"), [reg(3, 0, "A1"), ra1.at[1]], na // 2)
    got_a2[1, 1] = mv.remote(reg(3, 0, "A1"), a_half(ra2.at[1], 1), minus)
    yield
    for way in (0, 1):
        for h in (0, 1):
            got_b2[way, 0, h].wait_recv()
    got_p.wait_recv()
    add_blocks(out.at[pl.ds(na, nb)], [reg(0, 0, "B"), rb2.at[0, 0], rb2.at[1, 0], rp], nb)
    yield
    got_a[0].wait_recv()
    for way in (0, 1):
        for h in (0, 1):
            got_a2[way, h].wait_recv()
    add_blocks(out.at[pl.ds(0, na)], [reg(0, 0, "A"), ra.at[0], ra2.at[0], ra2.at[1]], na)


def spread_steps(plan, base, flip, tiles, source, staged, out, blocks, cuts):
    total = tiles.shape[0]
    perm, anchor, fresh, last, has = (functools.partial(lambda row, i: plan[row, i], base + j) for j in range(5))

    def body(i, acc):
        first = i * UNROLL
        prods = []
        for u in range(UNROLL):
            tile = tiles[perm(first + u)]
            other = source[anchor(first + u)]
            left, right = (other, tile) if flip else (tile, other)
            prods.append(jnp.dot(left, right, preferred_element_type=F32))
        for u in range(UNROLL):
            begins = jnp.full((SIDE, SIDE), fresh(first + u), jnp.int32) != 0
            acc = jnp.where(begins, 0.0, acc) + prods[u]
            staged[first + u] = acc.astype(BF16)
        return acc

    steps = total // UNROLL
    acc = jnp.zeros((SIDE, SIDE), F32)
    for cut in range(cuts):
        acc = lax.fori_loop(cut * steps // cuts, (cut + 1) * steps // cuts, body, acc)
        if cut < cuts - 1:
            yield

    group = 8

    def put(i, carry):
        for v in range(group):
            r = i * group + v
            filled = jnp.full((SIDE, SIDE), has(r), jnp.int32) != 0
            out[r] = jnp.where(filled, staged[last(r)].astype(F32), 0.0).astype(BF16)
        return carry

    lax.fori_loop(0, blocks // group, put, 0)


def reduce_steps(mv, gt, wr1, wr2, wg_ref, row_peers, col_peers, nodes):
    r0 = lax.axis_index("row")
    c0 = lax.axis_index("col")
    n_row, n_col = len(row_peers) + 1, len(col_peers) + 1
    depth = gt.shape[0] // n_col

    def strip(c):
        return pl.ds(pl.multiple_of(c * depth, depth), depth)

    first = [
        mv.remote(gt.at[strip((c0 + j) % n_col)], wr1.at[j], col_peers[j - 1])
        for j in range(1, n_col)
    ]
    yield
    for copy in first:
        copy.wait_recv()
    total = gt[strip(c0), :]
    for j in range(1, n_col):
        total = total + wr1[j]
    wr2[r0] = total
    second = [mv.remote(wr2.at[r0], wr2.at[r0], peer) for peer in row_peers]
    yield
    for copy in second:
        copy.wait_recv()
    total = wr2[0]
    for j in range(1, n_row):
        total = total + wr2[j]
    wg_ref[strip(c0), :] = total / jnp.sqrt(F32(nodes))
    third = [mv.remote(wg_ref.at[strip(c0)], wg_ref.at[strip(c0)], peer) for peer in col_peers]
    yield
    for copy in third:
        copy.wait_recv()


def advance(steps, count=None):
    taken = 0
    while count is None or taken < count:
        try:
            next(steps)
        except StopIteration:
            return False
        taken += 1
    return True


def braid(*streams):
    left = list(streams)
    while left:
        left = [s for s in left if advance(s, 1)]


def layer_kernel(
    nodes, plan, x_ref, w_ref, cot_ref, tiles_ref, act_ref, wg_ref, fg_ref,
    tiles, staged, panel0, panel1, part0, part1, met0, met1, back0, back1,
    hid0, hid1, delta, cot, fgt0, fgt1, gt, wr1, wr2, *rest
):
    f_bufs = (rest[0:6], rest[6:12])
    b_bufs = (rest[12:18], rest[18:24])
    mv = Mover(*rest[24:27])
    panel, part, met, back = (panel0, panel1), (part0, part1), (met0, met1), (back0, back1)
    hid, fgt = (hid0, hid1), (fgt0, fgt1)
    z, xh, xl, y, k = place()
    r0, c0 = lax.axis_index("row"), lax.axis_index("col")
    rows = cot.shape[0]
    blocks = rows // SIDE
    n_row, n_col = lax.axis_size("row"), lax.axis_size("col")

    row_slot = lambda p, q: p * 2 + q
    col_slot = lambda p, q: (q * 4 + p) * 2 + k
    row_links = Links(
        (row_device((z + 1) % 4, xh), row_device((z + 3) % 4, xh)),
        row_device(z, 1 - xh), z, xh, row_slot, blocks)
    col_links = Links(
        (col_device(xl, (y + 1) % 4, k), col_device(xl, (y + 3) % 4, k)),
        col_device(1 - xl, y, k), y, xl, col_slot, blocks)
    twin = col_device(xl, y, 1 - k)

    loads = [
        mv.local(x_ref.at[:, :, pl.ds(h * SIDE, SIDE)], row_links.part(panel[h], 0, 0)) for h in (0, 1)
    ]
    load_tiles = mv.local(tiles_ref, tiles)
    load_cot = mv.local(cot_ref, cot)
    row_peers = [((r0 + j) % n_row, c0) for j in range(1, n_row)]
    col_peers = [(r0, (c0 + j) % n_col) for j in range(1, n_col)]
    greet(row_peers + col_peers)

    gathers = [gather_steps(mv, row_links, panel[h], lambda ref: None) for h in (0, 1)]
    loads[0].wait()
    advance(gathers[0], 4)
    loads[1].wait()
    while advance(gathers[0], 1):
        advance(gathers[1], 1)
    load_tiles.wait()

    def twin_steps(h):
        crossing = {}
        for d, side in ORDER:
            piece = (y + d) % 4 + 4 * (xl if side == 0 else 1 - xl)
            from_part = part[h].at[pl.ds((piece * 2 + 1 - k) * blocks, blocks)]
            to_met = met[h].at[pl.ds(piece * blocks, blocks)]
            crossing[d, side] = (mv.remote(from_part, to_met, twin), to_met)

        def ready(d, side):
            copy, land = crossing[d, side]
            copy.wait_recv()
            ref = col_links.part(part[h], d, side)
            add_blocks(ref, [ref, land], blocks)

        yield from scatter_steps(mv, col_links, part[h], f_bufs[h], hid[h], ready)

    cuts = 8
    spread = [
        spread_steps(plan, 0, False, tiles, panel[h], staged, part[h], part[h].shape[0], cuts)
        for h in (0, 1)
    ]
    while advance(spread[0], 1):
        advance(gathers[1], 1)
    scatters = [twin_steps(h) for h in (0, 1)]
    advance(scatters[0], 4)
    while advance(gathers[1], 1):
        advance(scatters[0], 1)
    while advance(spread[1], 1):
        advance(scatters[0], 1)
    forward_sends = mv.take()
    advance(scatters[1], 8)
    braid(scatters[0], scatters[1])

    load_cot.wait()
    weight = w_ref[...]
    mine = col_links.piece(0, 0) * blocks

    def dense(i, carry):
        at = pl.ds(pl.multiple_of(i * SIDE, SIDE), SIDE)
        hidden = jnp.concatenate([hid0[i], hid1[i]], axis=1)
        pre = jnp.dot(hidden, weight, preferred_element_type=F32)
        sig = 1.0 / (1.0 + jnp.exp(-pre))
        act_ref[at, :] = (pre * sig).astype(BF16)
        d = (cot[at, :].astype(F32) * sig * (1.0 + pre * (1.0 - sig))).astype(BF16)
        delta[at, :] = d
        turned = lax.dot_general(
            weight, d, (((1,), (1,)), ((), ())), preferred_element_type=F32
        ).astype(BF16)
        for h in (0, 1):
            back[h][mine + i] = turned[h * SIDE:(h + 1) * SIDE]
        return carry

    lax.fori_loop(0, blocks, dense, 0)

    shares = [[], []]

    def arrived(h, ref):
        shares[h].append(mv.remote(ref, ref, twin))

    def gather_back(h):
        arrived(h, col_links.part(back[h], 0, 0))
        yield from gather_steps(mv, col_links, back[h], functools.partial(arrived, h))
        for share in shares[h]:
            yield
            share.wait_recv()

    gathers = [gather_back(h) for h in (0, 1)]
    advance(gathers[0], 1)
    for h in (0, 1):
        gt[h * SIDE:(h + 1) * SIDE, :] = lax.dot_general(
            hid[h][...].reshape(rows, SIDE), delta[...], (((0,), (0,)), ((), ())), preferred_element_type=F32
        )
    advance(gathers[0], 3)
    reduce = reduce_steps(mv, gt, wr1, wr2, wg_ref, row_peers, col_peers, nodes)
    while advance(gathers[0], 1):
        advance(gathers[1], 1)
    advance(reduce, 1)
    spread = [
        spread_steps(plan, 5, True, tiles, back[h], staged, panel[h], panel[h].shape[0], cuts)
        for h in (0, 1)
    ]
    for copy in forward_sends:
        copy.wait_send()
    while advance(spread[0], 1):
        advance(gathers[1], 1)
    scatters = [
        scatter_steps(mv, row_links, panel[h], b_bufs[h], fgt[h], lambda d, side: None) for h in (0, 1)
    ]
    advance(scatters[0], 9)
    while advance(gathers[1], 1):
        advance(scatters[0], 1)
    while advance(spread[1], 1):
        advance(scatters[0], 1)
    advance(scatters[1], 9)
    braid(scatters[0], scatters[1], reduce)

    def turn(i, carry):
        at = pl.ds(pl.multiple_of(i * SIDE, SIDE), SIDE)
        for h in (0, 1):
            fg_ref[at, h * SIDE:(h + 1) * SIDE] = fgt[h][i].T
        return carry

    lax.fori_loop(0, blocks, turn, 0)
    mv.drain()


def layer(plan, features, weight, cotangent, values, nodes):
    rows, width = features.shape
    total, size, _ = values.shape
    n_row, n_col = lax.axis_size("row"), lax.axis_size("col")
    any_spec = pl.BlockSpec(memory_space=pl.ANY)
    vmem = pl.BlockSpec(memory_space=pltpu.VMEM)
    blocks = rows // SIDE
    half = lambda count: [pltpu.VMEM((count * blocks, SIDE, SIDE), BF16)] * 2
    return pl.pallas_call(
        functools.partial(layer_kernel, nodes),
        out_shape=(
            jax.ShapeDtypeStruct((rows, width), BF16),
            jax.ShapeDtypeStruct((width, width), F32),
            jax.ShapeDtypeStruct((rows, width), BF16),
        ),
        in_specs=[pl.BlockSpec(memory_space=pltpu.SMEM), any_spec, vmem, any_spec, any_spec],
        out_specs=(vmem, vmem, vmem),
        scratch_shapes=[
            pltpu.VMEM((total, size, size), BF16),
            pltpu.VMEM((total, size, size), BF16),
            *half(n_row),
            *half(n_col),
            *half(n_col // 2),
            *half(n_col),
            *half(1),
            pltpu.VMEM((rows, width), BF16),
            pltpu.VMEM((rows, width), BF16),
            *half(1),
            pltpu.VMEM((width, width), F32),
            pltpu.VMEM((n_col, width // n_col, width), F32),
            pltpu.VMEM((n_row, width // n_col, width), F32),
            *(scatter_scratch(blocks) * 4),
            pltpu.SemaphoreType.DMA((280,)),
            pltpu.SemaphoreType.DMA((280,)),
            pltpu.SemaphoreType.DMA((4,)),
        ],
        compiler_params=pltpu.CompilerParams(
            collective_id=1, has_side_effects=True, vmem_limit_bytes=63 * 2**20
        ),
    )(plan, features.reshape(blocks, SIDE, width), weight, cotangent, values)


def sorted_slots(dest, anchor, count, blocks):
    total = dest.shape[0]
    slot = jnp.arange(total, dtype=jnp.int32)
    dest = jnp.where(slot < count, dest, blocks)
    key = dest * total + slot
    rank = jnp.sum((key[None, :] < key[:, None]).astype(jnp.int32), axis=1)
    here = rank[None, :] == slot[:, None]
    pick = lambda a: jnp.sum(jnp.where(here, a[None, :], 0), axis=1)
    ordered = pick(dest)
    before = jnp.sum((dest[None, :] < ordered[:, None]).astype(jnp.int32), axis=1)
    fresh = (before == slot).astype(jnp.int32)
    last = jnp.sum((dest[None, :] <= slot[:, None]).astype(jnp.int32), axis=1) - 1
    has = jnp.sum((dest[None, :] == slot[:, None]).astype(jnp.int32), axis=1)
    return [pick(slot), pick(anchor), fresh, jnp.maximum(last, 0), has]


def per_device(features, weight, cotangent, tile_values, tile_rows, tile_cols, tile_count):
    rows_idx = tile_rows[0, 0]
    cols_idx = tile_cols[0, 0]
    count = tile_count[0, 0]
    rows = features.shape[0]
    size = tile_values.shape[-1]
    n_row, n_col = lax.axis_size("row"), lax.axis_size("col")
    plan = jnp.stack(
        sorted_slots(rows_idx, cols_idx, count, rows * n_col // size)
        + sorted_slots(cols_idx, rows_idx, count, rows * n_row // size)
    )
    return layer(plan, features, weight, cotangent, tile_values[0, 0], rows * n_row * n_col)


def solution(mesh):
    return jax.shard_map(
        per_device,
        mesh=mesh,
        in_specs=(
            P(("col", "row"), None),
            P(),
            P(("row", "col"), None),
            P("row", "col", None, None, None),
            P("row", "col", None),
            P("row", "col", None),
            P("row", "col"),
        ),
        out_specs=(P(("row", "col"), None), P(), P(("col", "row"), None)),
        check_vma=False,
    )
```

```python
import functools

import jax
import jax.numpy as jnp
from jax import lax
from jax.experimental import pallas as pl
from jax.experimental.pallas import tpu as pltpu
from jax.sharding import PartitionSpec as P

BF16 = jnp.bfloat16
F32 = jnp.float32
UNROLL = 32
GATHER_SHARE = (2, 4)
SCATTER_SHARE = (4, 2)
SIDE = 128


def place():
    r = lax.axis_index("row")
    c = lax.axis_index("col")
    return r // 2, r % 2, c // 8, (c // 2) % 4, c % 2


def row_device(z, xh):
    return (z * 2 + xh, lax.axis_index("col"))


def col_device(xl, y, k):
    return (lax.axis_index("row"), xl * 8 + y * 2 + k)


def greet(peers):
    barrier = pltpu.get_barrier_semaphore()
    for peer in peers:
        pl.semaphore_signal(barrier, inc=1, device_id=peer, device_id_type=pl.DeviceIdType.MESH)
    pl.semaphore_wait(barrier, len(peers))


class Mover:
    def __init__(self, send_sem, recv_sem, local_sem):
        self.send_sem, self.recv_sem, self.local_sem = send_sem, recv_sem, local_sem
        self.started = 0
        self.kept = 0
        self.pending = []

    def remote(self, src, dst, device):
        at = self.started
        self.started += 1
        copy = pltpu.make_async_remote_copy(
            src_ref=src,
            dst_ref=dst,
            send_sem=self.send_sem.at[at],
            recv_sem=self.recv_sem.at[at],
            device_id=device,
            device_id_type=pl.DeviceIdType.MESH,
        )
        copy.start()
        self.pending.append(copy)
        return copy

    def local(self, src, dst):
        copy = pltpu.make_async_copy(src, dst, self.local_sem.at[self.kept])
        copy.start()
        self.kept += 1
        return copy

    def drain(self):
        for copy in self.take():
            copy.wait_send()

    def take(self):
        copies, self.pending = self.pending, []
        return copies


def add_blocks(dst, terms, blocks):
    kind = BF16 if len(terms) == 2 else F32
    group = 2 if blocks % 2 == 0 else 1

    def body(i, carry):
        for g in range(group):
            at = i * group + g
            total = terms[0][at].astype(kind)
            for term in terms[1:]:
                total = total + term[at].astype(kind)
            dst[at] = total.astype(dst.dtype)
        return carry

    lax.fori_loop(0, blocks // group, body, 0)


def split(blocks, share):
    first = blocks // share
    rest = blocks - first
    return {
        "A": (0, first),
        "A0": (0, first // 2),
        "A1": (first // 2, first // 2),
        "B": (first, rest),
        "B0": (first, rest // 2),
        "B1": (first + rest // 2, rest // 2),
    }


class Links:
    def __init__(self, ring, pair, p, q, slot, blocks):
        self.ring, self.pair, self.p, self.q, self.slot, self.blocks = ring, pair, p, q, slot, blocks

    def piece(self, d, side):
        return self.slot((self.p + d) % 4, self.q if side == 0 else 1 - self.q)

    def part(self, ref, d, side, name=None, share=2):
        start, size = split(self.blocks, share)[name] if name else (0, self.blocks)
        return ref.at[pl.ds(self.piece(d, side) * self.blocks + start, size)]


def gather_steps(mv, links, out, share, arrived):
    plus, minus = links.ring
    pair = links.pair
    reg = functools.partial(links.part, out, share=share)

    def go(d, side, name, device):
        return mv.remote(reg(d, side, name), reg(d, side, name), device)

    pair_b = go(0, 0, "B", pair)
    a_plus = go(0, 0, "A", plus)
    a_minus = go(0, 0, "A", minus)
    b_plus = go(0, 0, "B", plus)
    b_minus = go(0, 0, "B", minus)
    pair_a = [go(0, 0, "A", pair)]
    yield
    a_plus.wait_recv()
    ra_plus = go(3, 0, "A0", plus)
    pair_a.append(go(3, 0, "A", pair))
    a_minus.wait_recv()
    ra_minus = go(1, 0, "A1", minus)
    pair_a.append(go(1, 0, "A", pair))
    arrived(reg(3, 0, "A"))
    arrived(reg(1, 0, "A"))
    yield
    pair_b.wait_recv()
    pb_plus = go(0, 1, "B", plus)
    pb_minus = go(0, 1, "B", minus)
    arrived(reg(0, 1, "B"))
    yield
    b_plus.wait_recv()
    rb_plus = go(3, 0, "B0", plus)
    b_minus.wait_recv()
    rb_minus = go(1, 0, "B1", minus)
    arrived(reg(3, 0, "B"))
    arrived(reg(1, 0, "B"))
    yield
    ra_plus.wait_recv()
    pair_a.append(go(2, 0, "A0", pair))
    ra_minus.wait_recv()
    pair_a.append(go(2, 0, "A1", pair))
    arrived(reg(2, 0, "A"))
    yield
    pb_plus.wait_recv()
    rpb_plus = go(3, 1, "B0", plus)
    pb_minus.wait_recv()
    rpb_minus = go(1, 1, "B1", minus)
    arrived(reg(3, 1, "B"))
    arrived(reg(1, 1, "B"))
    yield
    rb_plus.wait_recv()
    rb_minus.wait_recv()
    arrived(reg(2, 0, "B"))
    for d, copy in zip((0, 3, 1), pair_a):
        yield
        copy.wait_recv()
        arrived(reg(d, 1, "A"))
    yield
    pair_a[3].wait_recv()
    pair_a[4].wait_recv()
    arrived(reg(2, 1, "A"))
    yield
    rpb_plus.wait_recv()
    rpb_minus.wait_recv()
    arrived(reg(2, 1, "B"))


def scatter_scratch(blocks, share):
    parts = split(blocks, share)
    first, rest = parts["A"][1], parts["B"][1]
    return [
        pltpu.VMEM((4, first, SIDE, SIDE), BF16),
        pltpu.VMEM((2, 2, rest // 2, SIDE, SIDE), BF16),
        pltpu.VMEM((2, 2, rest, SIDE, SIDE), BF16),
        pltpu.VMEM((2, first // 2, SIDE, SIDE), BF16),
        pltpu.VMEM((2, first, SIDE, SIDE), BF16),
        pltpu.VMEM((rest, SIDE, SIDE), BF16),
    ]


ORDER = ((2, 1), (2, 0), (1, 1), (3, 1), (1, 0), (3, 0), (0, 1), (0, 0))


def scatter_steps(mv, links, held, share, bufs, out, ready):
    parts = split(links.blocks, share)
    plus, minus = links.ring
    pair = links.pair
    ra, rb1, rb2, ra1, ra2, rp = bufs
    nb, na = parts["B"][1], parts["A"][1]
    reg = functools.partial(links.part, held, share=share)
    b_half = lambda ref, h: ref.at[pl.ds(h * (nb // 2), nb // 2)]
    a_half = lambda ref, h: ref.at[pl.ds(h * (na // 2), na // 2)]
    got_b1, got_b2, got_a, got_a2 = {}, {}, {}, {}
    for d, side in ORDER:
        yield
        ready(d, side)
        if d == 2:
            got_b1[0, side] = mv.remote(reg(2, side, "B0"), rb1.at[0, side], plus)
            got_b1[1, side] = mv.remote(reg(2, side, "B1"), rb1.at[1, side], minus)
        elif d == 1:
            got_b2[0, side, 1] = mv.remote(reg(1, side, "B1"), b_half(rb2.at[0, side], 1), plus)
        elif d == 3:
            got_b2[1, side, 0] = mv.remote(reg(3, side, "B0"), b_half(rb2.at[1, side], 0), minus)
        if side == 1:
            got_a[d] = mv.remote(reg(d, 1, "A"), ra.at[d], pair)
    for side in (1, 0):
        yield
        got_b1[0, side].wait_recv()
        add_blocks(reg(1, side, "B0"), [reg(1, side, "B0"), rb1.at[0, side]], nb // 2)
        got_b2[0, side, 0] = mv.remote(reg(1, side, "B0"), b_half(rb2.at[0, side], 0), plus)
        got_b1[1, side].wait_recv()
        add_blocks(reg(3, side, "B1"), [reg(3, side, "B1"), rb1.at[1, side]], nb // 2)
        got_b2[1, side, 1] = mv.remote(reg(3, side, "B1"), b_half(rb2.at[1, side], 1), minus)
    yield
    got_a[2].wait_recv()
    add_blocks(reg(2, 0, "A"), [reg(2, 0, "A"), ra.at[2]], na)
    got_a1 = [
        mv.remote(reg(2, 0, "A0"), ra1.at[0], plus),
        mv.remote(reg(2, 0, "A1"), ra1.at[1], minus),
    ]
    yield
    got_a[1].wait_recv()
    add_blocks(reg(1, 0, "A"), [reg(1, 0, "A"), ra.at[1]], na)
    got_a2[0, 1] = mv.remote(reg(1, 0, "A1"), a_half(ra2.at[0], 1), plus)
    got_a[3].wait_recv()
    add_blocks(reg(3, 0, "A"), [reg(3, 0, "A"), ra.at[3]], na)
    got_a2[1, 0] = mv.remote(reg(3, 0, "A0"), a_half(ra2.at[1], 0), minus)
    yield
    for way in (0, 1):
        for h in (0, 1):
            got_b2[way, 1, h].wait_recv()
    add_blocks(reg(0, 1, "B"), [reg(0, 1, "B"), rb2.at[0, 1], rb2.at[1, 1]], nb)
    got_p = mv.remote(reg(0, 1, "B"), rp, pair)
    yield
    got_a1[0].wait_recv()
    add_blocks(reg(1, 0, "A0"), [reg(1, 0, "A0"), ra1.at[0]], na // 2)
    got_a2[0, 0] = mv.remote(reg(1, 0, "A0"), a_half(ra2.at[0], 0), plus)
    got_a1[1].wait_recv()
    add_blocks(reg(3, 0, "A1"), [reg(3, 0, "A1"), ra1.at[1]], na // 2)
    got_a2[1, 1] = mv.remote(reg(3, 0, "A1"), a_half(ra2.at[1], 1), minus)
    yield
    for way in (0, 1):
        for h in (0, 1):
            got_b2[way, 0, h].wait_recv()
    got_p.wait_recv()
    add_blocks(out.at[pl.ds(na, nb)], [reg(0, 0, "B"), rb2.at[0, 0], rb2.at[1, 0], rp], nb)
    yield
    got_a[0].wait_recv()
    for way in (0, 1):
        for h in (0, 1):
            got_a2[way, h].wait_recv()
    add_blocks(out.at[pl.ds(0, na)], [reg(0, 0, "A"), ra.at[0], ra2.at[0], ra2.at[1]], na)


def spread_steps(plan, which, flip, tiles, source, staged, out, cuts):
    read = lambda row: lambda i: plan[which, row, i]
    tile0, tile1, anchor0, anchor1, fresh, last, has = (read(row) for row in range(7))

    def body(i, acc):
        first = i * UNROLL
        prods = []
        for u in range(UNROLL):
            at = first + u
            pair = (tiles[tile0(at)], tiles[tile1(at)])
            other = (source[anchor0(at)], source[anchor1(at)])
            left, right = (other, pair) if flip else (pair, other)
            prods.append(
                jnp.dot(
                    jnp.concatenate(left, axis=1),
                    jnp.concatenate(right, axis=0),
                    preferred_element_type=F32,
                )
            )
        for u in range(UNROLL):
            begins = jnp.full((SIDE, SIDE), fresh(first + u), jnp.int32) != 0
            acc = jnp.where(begins, 0.0, acc) + prods[u]
            staged[first + u] = acc.astype(BF16)
        return acc

    blocks = out.shape[0]
    steps = pair_slots(tiles.shape[0] - 1, blocks) // UNROLL
    acc = jnp.zeros((SIDE, SIDE), F32)
    for cut in range(cuts):
        acc = lax.fori_loop(cut * steps // cuts, (cut + 1) * steps // cuts, body, acc)
        if cut < cuts - 1:
            yield

    group = 8

    def put(i, carry):
        for v in range(group):
            r = i * group + v
            filled = jnp.full((SIDE, SIDE), has(r), jnp.int32) != 0
            out[r] = jnp.where(filled, staged[last(r)].astype(F32), 0.0).astype(BF16)
        return carry

    lax.fori_loop(0, blocks // group, put, 0)


def reduce_steps(mv, gt, met_rows, met_strips, strips, wg_ref, halvings, doublings, nodes):
    start, size = 0, gt.shape[0]
    rows = lambda start, size: pl.ds(pl.multiple_of(start, 8), size)
    for i, (device, bit) in enumerate(halvings):
        size //= 2
        land = met_rows.at[pl.ds(size, size)]
        copy = mv.remote(gt.at[rows(start + (1 - bit) * size, size)], land, device)
        start = start + bit * size
        yield
        copy.wait_recv()
        keep = rows(start, size)
        gt[keep, :] = gt[keep, :] + land[...]
    strips[0] = gt[rows(start, size), :]
    for i, device in enumerate(doublings):
        copy = mv.remote(strips.at[i], met_strips.at[i], device)
        yield
        copy.wait_recv()
        strips[i + 1] = strips[i] + met_strips[i]
    wg_ref[rows(start, size), :] = strips[len(doublings)] / jnp.sqrt(F32(nodes))
    for device, bit in reversed(halvings):
        copy = mv.remote(wg_ref.at[rows(start, size)], wg_ref.at[rows(start, size)], device)
        yield
        copy.wait_recv()
        start = start - bit * size
        size *= 2


def advance(steps, count=None):
    taken = 0
    while count is None or taken < count:
        try:
            next(steps)
        except StopIteration:
            return False
        taken += 1
    return True


def braid(*streams):
    left = list(streams)
    while left:
        left = [s for s in left if advance(s, 1)]


def both(main, other):
    for step in main:
        advance(other, 1)
        yield step


def weave(gather, scatter, spread):
    advance(scatter, 1)
    advance(gather, 1)
    advance(scatter, 2)
    advance(gather, 1)
    advance(scatter, 4)
    advance(gather, 1)
    advance(scatter, 2)
    advance(gather, 2)
    advance(scatter, 1)
    advance(gather)
    while advance(spread, 1):
        advance(scatter, 1)


def weave_ends(early, late, sends):
    advance(late, 5)
    advance(early, 1)
    advance(late, 4)
    for copy in sends:
        copy.wait_send()
    braid(early, late)


def layer_kernel(
    nodes, plan, x_ref, w_ref, cot_ref, tiles_ref, act_ref, wg_ref, fgt0, fgt1,
    tiles, staged, panel0, panel1, part0, part1, met0, met1, back0, back1,
    hid0, hid1, delta, cot, gt, met_rows, met_strips, strips, *rest
):
    f_bufs = (rest[0:6], rest[6:12])
    b_bufs = (rest[12:18], rest[18:24])
    mv = Mover(*rest[24:27])
    panel, part, met, back = (panel0, panel1), (part0, part1), (met0, met1), (back0, back1)
    hid, fgt = (hid0, hid1), (fgt0, fgt1)
    z, xh, xl, y, k = place()
    rows = cot.shape[0]
    blocks = rows // SIDE

    row_slot = lambda p, q: p * 2 + q
    col_slot = lambda p, q: (q * 4 + p) * 2 + k
    row_links = Links(
        (row_device((z + 1) % 4, xh), row_device((z + 3) % 4, xh)),
        row_device(z, 1 - xh), z, xh, row_slot, blocks)
    col_links = Links(
        (col_device(xl, (y + 1) % 4, k), col_device(xl, (y + 3) % 4, k)),
        col_device(1 - xl, y, k), y, xl, col_slot, blocks)
    twin = col_device(xl, y, 1 - k)

    loads = [
        mv.local(x_ref.at[:, :, pl.ds(h * SIDE, SIDE)], row_links.part(panel[h], 0, 0)) for h in (0, 1)
    ]
    count = tiles_ref.shape[0]
    load_tiles = mv.local(tiles_ref, tiles.at[pl.ds(0, count)])
    tiles[count] = jnp.zeros((SIDE, SIDE), BF16)
    load_cot = mv.local(cot_ref, cot)
    greet([*row_links.ring, row_links.pair, *col_links.ring, col_links.pair, twin])

    gathers = [gather_steps(mv, row_links, panel[h], GATHER_SHARE[h], lambda ref: None) for h in (0, 1)]
    loads[0].wait()
    advance(gathers[0], 7)
    loads[1].wait()
    advance(gathers[1], 1)
    advance(gathers[0])
    load_tiles.wait()

    def twin_steps(h):
        crossing = {}
        to_cross = list(ORDER)

        def cross(count):
            for d, side in to_cross[:count]:
                piece = (y + d) % 4 + 4 * (xl if side == 0 else 1 - xl)
                from_part = part[h].at[pl.ds((piece * 2 + 1 - k) * blocks, blocks)]
                to_met = met[h].at[pl.ds(piece * blocks, blocks)]
                crossing[d, side] = (mv.remote(from_part, to_met, twin), to_met)
            del to_cross[:count]

        cross(3)

        def ready(d, side):
            cross(1)
            copy, land = crossing[d, side]
            copy.wait_recv()
            ref = col_links.part(part[h], d, side)
            add_blocks(ref, [ref, land], blocks)

        yield from scatter_steps(mv, col_links, part[h], SCATTER_SHARE[h], f_bufs[h], hid[h], ready)

    cuts = 4
    spread = [
        spread_steps(plan, 0, False, tiles, panel[h], staged, part[h], cuts)
        for h in (0, 1)
    ]
    advance(spread[0], 2)
    advance(gathers[1], 1)
    advance(spread[0], 1)
    advance(gathers[1], 1)
    advance(spread[0])
    scatters = [twin_steps(h) for h in (0, 1)]
    weave(gathers[1], scatters[0], spread[1])
    forward_sends = mv.take()
    weave_ends(scatters[0], scatters[1], [])

    load_cot.wait()
    weight = w_ref[...]
    mine = col_links.piece(0, 0) * blocks

    def dense(i, carry):
        at = pl.ds(pl.multiple_of(i * SIDE, SIDE), SIDE)
        hidden = jnp.concatenate([hid0[i], hid1[i]], axis=1)
        pre = jnp.dot(hidden, weight, preferred_element_type=F32)
        sig = 1.0 / (1.0 + jnp.exp(-pre))
        act_ref[at, :] = (pre * sig).astype(BF16)
        d = (cot[at, :].astype(F32) * sig * (1.0 + pre * (1.0 - sig))).astype(BF16)
        delta[at, :] = d
        turned = lax.dot_general(
            weight, d, (((1,), (1,)), ((), ())), preferred_element_type=F32
        ).astype(BF16)
        for h in (0, 1):
            back[h][mine + i] = turned[h * SIDE:(h + 1) * SIDE]
        return carry

    lax.fori_loop(0, blocks, dense, 0)

    shares = [[], []]

    def arrived(h, ref):
        shares[h].append(mv.remote(ref, ref, twin))

    def gather_back(h):
        arrived(h, col_links.part(back[h], 0, 0))
        yield from gather_steps(mv, col_links, back[h], GATHER_SHARE[h], functools.partial(arrived, h))
        yield
        for share in shares[h]:
            share.wait_recv()

    gathers = [gather_back(h) for h in (0, 1)]
    advance(gathers[0], 1)
    for h in (0, 1):
        gt[h * SIDE:(h + 1) * SIDE, :] = lax.dot_general(
            hid[h][...].reshape(rows, SIDE), delta[...], (((0,), (0,)), ((), ())), preferred_element_type=F32
        )
    for copy in forward_sends:
        copy.wait_send()
    advance(gathers[0], 6)
    near = lambda i: i + 1 - 2 * (i % 2)
    halvings = (
        (twin, k),
        (col_links.pair, xl),
        (col_device(xl, near(y), k), (y + 1) // 2 % 2),
        (col_device(xl, 3 - y, k), y // 2),
    )
    doublings = (row_links.pair, row_device(near(z), xh), row_device(3 - z, xh))
    reduce = reduce_steps(mv, gt, met_rows, met_strips, strips, wg_ref, halvings, doublings, nodes)
    advance(reduce, 1)
    advance(gathers[1], 1)
    advance(gathers[0])
    spread = [
        spread_steps(plan, 1, True, tiles, back[h], staged, panel[h], cuts) for h in (0, 1)
    ]
    advance(spread[0], 2)
    advance(gathers[1], 1)
    advance(reduce, 1)
    advance(spread[0], 1)
    advance(gathers[1], 1)
    advance(reduce, 1)
    advance(spread[0])
    scatters = [
        scatter_steps(mv, row_links, panel[h], SCATTER_SHARE[h], b_bufs[h], fgt[h], lambda d, side: None) for h in (0, 1)
    ]
    weave(gathers[1], scatters[0], both(spread[1], reduce))
    backward_sends = mv.take()
    weave_ends(scatters[0], both(scatters[1], reduce), backward_sends)
    advance(reduce)

    mv.drain()


def layer(plan, features, weight, cotangent, values, nodes):
    rows, width = features.shape
    total, size, _ = values.shape
    n_row, n_col = lax.axis_size("row"), lax.axis_size("col")
    any_spec = pl.BlockSpec(memory_space=pl.ANY)
    vmem = pl.BlockSpec(memory_space=pltpu.VMEM)
    blocks = rows // SIDE
    half = lambda count: [pltpu.VMEM((count * blocks, SIDE, SIDE), BF16)] * 2
    return pl.pallas_call(
        functools.partial(layer_kernel, nodes),
        out_shape=(
            jax.ShapeDtypeStruct((rows, width), BF16),
            jax.ShapeDtypeStruct((width, width), F32),
            *[jax.ShapeDtypeStruct((blocks, SIDE, SIDE), BF16)] * 2,
        ),
        in_specs=[pl.BlockSpec(memory_space=pltpu.SMEM), any_spec, vmem, any_spec, any_spec],
        out_specs=(vmem,) * 4,
        scratch_shapes=[
            pltpu.VMEM((total + 1, size, size), BF16),
            pltpu.VMEM((pair_slots(total, n_col * blocks), size, size), BF16),
            *half(n_row),
            *half(n_col),
            *half(n_col // 2),
            *half(n_col),
            *half(1),
            pltpu.VMEM((rows, width), BF16),
            pltpu.VMEM((rows, width), BF16),
            pltpu.VMEM((width, width), F32),
            pltpu.VMEM((width, width), F32),
            pltpu.VMEM((3, width // n_col, width), F32),
            pltpu.VMEM((4, width // n_col, width), F32),
            *((scatter_scratch(blocks, SCATTER_SHARE[0]) + scatter_scratch(blocks, SCATTER_SHARE[1])) * 2),
            pltpu.SemaphoreType.DMA((280,)),
            pltpu.SemaphoreType.DMA((280,)),
            pltpu.SemaphoreType.DMA((4,)),
        ],
        compiler_params=pltpu.CompilerParams(
            collective_id=1, has_side_effects=True, vmem_limit_bytes=63 * 2**20
        ),
    )(plan, features.reshape(blocks, SIDE, width), weight, cotangent, values)


def unfold_kernel(act_ref, wg_ref, fgt0, fgt1, act_out, wg_out, fg_out):
    def body(i, carry):
        at = pl.ds(pl.multiple_of(i * SIDE, SIDE), SIDE)
        act_out[at, :] = act_ref[at, :]
        fg_out[at, :] = jnp.concatenate([fgt0[i].T, fgt1[i].T], axis=1)
        return carry

    lax.fori_loop(0, fgt0.shape[0], body, 0)
    wg_out[...] = wg_ref[...]


def unfold(activated, weight_grad, turned0, turned1):
    vmem = pl.BlockSpec(memory_space=pltpu.VMEM)
    like = lambda a: jax.ShapeDtypeStruct(a.shape, a.dtype)
    return pl.pallas_call(
        unfold_kernel,
        out_shape=(like(activated), like(weight_grad), like(activated)),
        in_specs=[vmem] * 4,
        out_specs=(vmem,) * 3,
    )(activated, weight_grad, turned0, turned1)


def pair_slots(total, blocks):
    need = (total + blocks) // 2
    return -(-need // UNROLL) * UNROLL


def paired_slots(dest, anchor, count, blocks, room):
    total = dest.shape[0]
    slot = jnp.arange(total, dtype=jnp.int32)
    block = jnp.arange(room, dtype=jnp.int32)
    add = lambda hit, value=1: jnp.sum(jnp.where(hit, value, 0), axis=1, dtype=jnp.int32)
    live = slot < count
    dest = jnp.where(live, dest, blocks)
    mine = add(dest[None, :] == block[:, None])
    pairs = (mine + 1) // 2
    start = add(block[None, :] < block[:, None], pairs[None, :])
    order = add((dest[None, :] == dest[:, None]) & (slot[None, :] < slot[:, None]))
    begin = add(dest[:, None] == block[None, :], start[None, :])
    at = jnp.where(live, begin + order // 2, room)
    here = at[None, :] == block[:, None]
    first = here & (order % 2 == 0)[None, :]
    second = here & (order % 2 == 1)[None, :]
    alone = 1 - add(second)
    tile0 = add(first, slot[None, :])
    tile1 = add(second, slot[None, :]) + alone * total
    anchor0 = add(first, anchor[None, :])
    anchor1 = add(second, anchor[None, :]) + alone * anchor0
    fresh = add(first & (order == 0)[None, :])
    return jnp.stack([tile0, tile1, anchor0, anchor1, fresh, jnp.maximum(start + pairs - 1, 0), mine])


def per_device(features, weight, cotangent, tile_values, tile_rows, tile_cols, tile_count):
    rows_idx = tile_rows[0, 0]
    cols_idx = tile_cols[0, 0]
    count = tile_count[0, 0]
    rows = features.shape[0]
    size = tile_values.shape[-1]
    n_row, n_col = lax.axis_size("row"), lax.axis_size("col")
    row_blocks, col_blocks = rows * n_col // size, rows * n_row // size
    room = pair_slots(rows_idx.shape[0], row_blocks)
    plan = jax.vmap(paired_slots, in_axes=(0, 0, None, 0, None))(
        jnp.stack([rows_idx, cols_idx]),
        jnp.stack([cols_idx, rows_idx]),
        count,
        jnp.array([row_blocks, col_blocks], jnp.int32),
        room,
    )
    return unfold(*layer(plan, features, weight, cotangent, tile_values[0, 0], rows * n_row * n_col))


def solution(mesh):
    return jax.shard_map(
        per_device,
        mesh=mesh,
        in_specs=(
            P(("col", "row"), None),
            P(),
            P(("row", "col"), None),
            P("row", "col", None, None, None),
            P("row", "col", None),
            P("row", "col", None),
            P("row", "col"),
        ),
        out_specs=(P(("row", "col"), None), P(), P(("col", "row"), None)),
        check_vma=False,
    )
```

```python
import functools

import jax
import jax.numpy as jnp
from jax import lax
from jax.experimental import pallas as pl
from jax.experimental.pallas import tpu as pltpu
from jax.sharding import PartitionSpec as P

BF16 = jnp.bfloat16
F32 = jnp.float32
UNROLL = 32
GATHER_SHARE = (2, 4)
SCATTER_SHARE = (4, 2)
SIDE = 128


def place():
    r = lax.axis_index("row")
    c = lax.axis_index("col")
    return r // 2, r % 2, c // 8, (c // 2) % 4, c % 2


def row_device(z, xh):
    return (z * 2 + xh, lax.axis_index("col"))


def col_device(xl, y, k):
    return (lax.axis_index("row"), xl * 8 + y * 2 + k)


def greet(peers):
    barrier = pltpu.get_barrier_semaphore()
    for peer in peers:
        pl.semaphore_signal(barrier, inc=1, device_id=peer, device_id_type=pl.DeviceIdType.MESH)
    pl.semaphore_wait(barrier, len(peers))


class Mover:
    def __init__(self, send_sem, recv_sem, local_sem):
        self.send_sem, self.recv_sem, self.local_sem = send_sem, recv_sem, local_sem
        self.started = 0
        self.kept = 0
        self.pending = []

    def remote(self, src, dst, device):
        at = self.started
        self.started += 1
        copy = pltpu.make_async_remote_copy(
            src_ref=src,
            dst_ref=dst,
            send_sem=self.send_sem.at[at],
            recv_sem=self.recv_sem.at[at],
            device_id=device,
            device_id_type=pl.DeviceIdType.MESH,
        )
        copy.start()
        self.pending.append(copy)
        return copy

    def local(self, src, dst):
        copy = pltpu.make_async_copy(src, dst, self.local_sem.at[self.kept])
        copy.start()
        self.kept += 1
        return copy

    def drain(self):
        for copy in self.take():
            copy.wait_send()

    def take(self):
        copies, self.pending = self.pending, []
        return copies


def add_blocks(dst, terms, blocks):
    kind = BF16 if len(terms) == 2 else F32
    group = 2 if blocks % 2 == 0 else 1

    def body(i, carry):
        for g in range(group):
            at = i * group + g
            total = terms[0][at].astype(kind)
            for term in terms[1:]:
                total = total + term[at].astype(kind)
            dst[at] = total.astype(dst.dtype)
        return carry

    lax.fori_loop(0, blocks // group, body, 0)


def split(blocks, share):
    first = blocks // share
    rest = blocks - first
    return {
        "A": (0, first),
        "A0": (0, first // 2),
        "A1": (first // 2, first // 2),
        "B": (first, rest),
        "B0": (first, rest // 2),
        "B1": (first + rest // 2, rest // 2),
    }


class Links:
    def __init__(self, ring, pair, p, q, slot, blocks):
        self.ring, self.pair, self.p, self.q, self.slot, self.blocks = ring, pair, p, q, slot, blocks

    def piece(self, d, side):
        return self.slot((self.p + d) % 4, self.q if side == 0 else 1 - self.q)

    def part(self, ref, d, side, name=None, share=2):
        start, size = split(self.blocks, share)[name] if name else (0, self.blocks)
        return ref.at[pl.ds(self.piece(d, side) * self.blocks + start, size)]


def gather_steps(mv, links, out, share, arrived):
    plus, minus = links.ring
    pair = links.pair
    reg = functools.partial(links.part, out, share=share)

    def go(d, side, name, device):
        return mv.remote(reg(d, side, name), reg(d, side, name), device)

    pair_b = go(0, 0, "B", pair)
    a_plus = go(0, 0, "A", plus)
    a_minus = go(0, 0, "A", minus)
    b_plus = go(0, 0, "B", plus)
    b_minus = go(0, 0, "B", minus)
    pair_a = [go(0, 0, "A", pair)]
    yield
    a_plus.wait_recv()
    ra_plus = go(3, 0, "A0", plus)
    pair_a.append(go(3, 0, "A", pair))
    a_minus.wait_recv()
    ra_minus = go(1, 0, "A1", minus)
    pair_a.append(go(1, 0, "A", pair))
    arrived(reg(3, 0, "A"))
    arrived(reg(1, 0, "A"))
    yield
    pair_b.wait_recv()
    pb_plus = go(0, 1, "B", plus)
    pb_minus = go(0, 1, "B", minus)
    arrived(reg(0, 1, "B"))
    yield
    b_plus.wait_recv()
    rb_plus = go(3, 0, "B0", plus)
    b_minus.wait_recv()
    rb_minus = go(1, 0, "B1", minus)
    arrived(reg(3, 0, "B"))
    arrived(reg(1, 0, "B"))
    yield
    ra_plus.wait_recv()
    pair_a.append(go(2, 0, "A0", pair))
    ra_minus.wait_recv()
    pair_a.append(go(2, 0, "A1", pair))
    arrived(reg(2, 0, "A"))
    yield
    pb_plus.wait_recv()
    rpb_plus = go(3, 1, "B0", plus)
    pb_minus.wait_recv()
    rpb_minus = go(1, 1, "B1", minus)
    arrived(reg(3, 1, "B"))
    arrived(reg(1, 1, "B"))
    yield
    rb_plus.wait_recv()
    rb_minus.wait_recv()
    arrived(reg(2, 0, "B"))
    for d, copy in zip((0, 3, 1), pair_a):
        yield
        copy.wait_recv()
        arrived(reg(d, 1, "A"))
    yield
    pair_a[3].wait_recv()
    pair_a[4].wait_recv()
    arrived(reg(2, 1, "A"))
    yield
    rpb_plus.wait_recv()
    rpb_minus.wait_recv()
    arrived(reg(2, 1, "B"))


def scatter_scratch(blocks, share):
    parts = split(blocks, share)
    first, rest = parts["A"][1], parts["B"][1]
    return [
        pltpu.VMEM((4, first, SIDE, SIDE), BF16),
        pltpu.VMEM((2, 2, rest // 2, SIDE, SIDE), BF16),
        pltpu.VMEM((2, 2, rest, SIDE, SIDE), BF16),
        pltpu.VMEM((2, first // 2, SIDE, SIDE), BF16),
        pltpu.VMEM((2, first, SIDE, SIDE), BF16),
        pltpu.VMEM((rest, SIDE, SIDE), BF16),
    ]


ORDER = ((2, 1), (2, 0), (1, 1), (3, 1), (1, 0), (3, 0), (0, 1), (0, 0))


def scatter_steps(mv, links, held, share, bufs, out, ready):
    parts = split(links.blocks, share)
    plus, minus = links.ring
    pair = links.pair
    ra, rb1, rb2, ra1, ra2, rp = bufs
    nb, na = parts["B"][1], parts["A"][1]
    reg = functools.partial(links.part, held, share=share)
    b_half = lambda ref, h: ref.at[pl.ds(h * (nb // 2), nb // 2)]
    a_half = lambda ref, h: ref.at[pl.ds(h * (na // 2), na // 2)]
    got_b1, got_b2, got_a, got_a2 = {}, {}, {}, {}
    for d, side in ORDER:
        yield
        ready(d, side)
        if d == 2:
            got_b1[0, side] = mv.remote(reg(2, side, "B0"), rb1.at[0, side], plus)
            got_b1[1, side] = mv.remote(reg(2, side, "B1"), rb1.at[1, side], minus)
        elif d == 1:
            got_b2[0, side, 1] = mv.remote(reg(1, side, "B1"), b_half(rb2.at[0, side], 1), plus)
        elif d == 3:
            got_b2[1, side, 0] = mv.remote(reg(3, side, "B0"), b_half(rb2.at[1, side], 0), minus)
        if side == 1:
            got_a[d] = mv.remote(reg(d, 1, "A"), ra.at[d], pair)
    for side in (1, 0):
        yield
        got_b1[0, side].wait_recv()
        add_blocks(reg(1, side, "B0"), [reg(1, side, "B0"), rb1.at[0, side]], nb // 2)
        got_b2[0, side, 0] = mv.remote(reg(1, side, "B0"), b_half(rb2.at[0, side], 0), plus)
        got_b1[1, side].wait_recv()
        add_blocks(reg(3, side, "B1"), [reg(3, side, "B1"), rb1.at[1, side]], nb // 2)
        got_b2[1, side, 1] = mv.remote(reg(3, side, "B1"), b_half(rb2.at[1, side], 1), minus)
    yield
    got_a[2].wait_recv()
    add_blocks(reg(2, 0, "A"), [reg(2, 0, "A"), ra.at[2]], na)
    got_a1 = [
        mv.remote(reg(2, 0, "A0"), ra1.at[0], plus),
        mv.remote(reg(2, 0, "A1"), ra1.at[1], minus),
    ]
    yield
    got_a[1].wait_recv()
    add_blocks(reg(1, 0, "A"), [reg(1, 0, "A"), ra.at[1]], na)
    got_a2[0, 1] = mv.remote(reg(1, 0, "A1"), a_half(ra2.at[0], 1), plus)
    got_a[3].wait_recv()
    add_blocks(reg(3, 0, "A"), [reg(3, 0, "A"), ra.at[3]], na)
    got_a2[1, 0] = mv.remote(reg(3, 0, "A0"), a_half(ra2.at[1], 0), minus)
    yield
    for way in (0, 1):
        for h in (0, 1):
            got_b2[way, 1, h].wait_recv()
    add_blocks(reg(0, 1, "B"), [reg(0, 1, "B"), rb2.at[0, 1], rb2.at[1, 1]], nb)
    got_p = mv.remote(reg(0, 1, "B"), rp, pair)
    yield
    got_a1[0].wait_recv()
    add_blocks(reg(1, 0, "A0"), [reg(1, 0, "A0"), ra1.at[0]], na // 2)
    got_a2[0, 0] = mv.remote(reg(1, 0, "A0"), a_half(ra2.at[0], 0), plus)
    got_a1[1].wait_recv()
    add_blocks(reg(3, 0, "A1"), [reg(3, 0, "A1"), ra1.at[1]], na // 2)
    got_a2[1, 1] = mv.remote(reg(3, 0, "A1"), a_half(ra2.at[1], 1), minus)
    yield
    for way in (0, 1):
        for h in (0, 1):
            got_b2[way, 0, h].wait_recv()
    got_p.wait_recv()
    add_blocks(out.at[pl.ds(na, nb)], [reg(0, 0, "B"), rb2.at[0, 0], rb2.at[1, 0], rp], nb)
    yield
    got_a[0].wait_recv()
    for way in (0, 1):
        for h in (0, 1):
            got_a2[way, h].wait_recv()
    add_blocks(out.at[pl.ds(0, na)], [reg(0, 0, "A"), ra.at[0], ra2.at[0], ra2.at[1]], na)


def spread_steps(plan, which, flip, tiles, source, staged, out, cuts):
    read = lambda row: lambda i: plan[which, row, i]
    tile0, tile1, anchor0, anchor1, fresh, last, has = (read(row) for row in range(7))

    def body(i, acc):
        first = i * UNROLL
        prods = []
        for u in range(UNROLL):
            at = first + u
            pair = (tiles[tile0(at)], tiles[tile1(at)])
            other = (source[anchor0(at)], source[anchor1(at)])
            left, right = (other, pair) if flip else (pair, other)
            prods.append(
                jnp.dot(
                    jnp.concatenate(left, axis=1),
                    jnp.concatenate(right, axis=0),
                    preferred_element_type=F32,
                )
            )
        for u in range(UNROLL):
            begins = jnp.full((SIDE, SIDE), fresh(first + u), jnp.int32) != 0
            acc = jnp.where(begins, 0.0, acc) + prods[u]
            staged[first + u] = acc.astype(BF16)
        return acc

    blocks = out.shape[0]
    steps = pair_slots(tiles.shape[0] - 1, blocks) // UNROLL
    acc = jnp.zeros((SIDE, SIDE), F32)
    for cut in range(cuts):
        acc = lax.fori_loop(cut * steps // cuts, (cut + 1) * steps // cuts, body, acc)
        if cut < cuts - 1:
            yield

    group = 8

    def put(i, carry):
        for v in range(group):
            r = i * group + v
            filled = jnp.full((SIDE, SIDE), has(r), jnp.int32) != 0
            out[r] = jnp.where(filled, staged[last(r)].astype(F32), 0.0).astype(BF16)
        return carry

    lax.fori_loop(0, blocks // group, put, 0)


def reduce_steps(mv, gt, met_rows, met_strips, strips, wg_ref, halvings, doublings, nodes):
    start, size = 0, gt.shape[0]
    rows = lambda start, size: pl.ds(pl.multiple_of(start, 8), size)
    for i, (device, bit) in enumerate(halvings):
        size //= 2
        land = met_rows.at[pl.ds(size, size)]
        copy = mv.remote(gt.at[rows(start + (1 - bit) * size, size)], land, device)
        start = start + bit * size
        yield
        copy.wait_recv()
        keep = rows(start, size)
        gt[keep, :] = gt[keep, :] + land[...]
    strips[0] = gt[rows(start, size), :]
    for i, device in enumerate(doublings):
        copy = mv.remote(strips.at[i], met_strips.at[i], device)
        yield
        copy.wait_recv()
        strips[i + 1] = strips[i] + met_strips[i]
    wg_ref[rows(start, size), :] = strips[len(doublings)] / jnp.sqrt(F32(nodes))
    for device, bit in reversed(halvings):
        copy = mv.remote(wg_ref.at[rows(start, size)], wg_ref.at[rows(start, size)], device)
        yield
        copy.wait_recv()
        start = start - bit * size
        size *= 2


def advance(steps, count=None):
    taken = 0
    while count is None or taken < count:
        try:
            next(steps)
        except StopIteration:
            return False
        taken += 1
    return True


def braid(*streams):
    left = list(streams)
    while left:
        left = [s for s in left if advance(s, 1)]


def both(main, other):
    for step in main:
        advance(other, 1)
        yield step


def weave(gather, scatter, spread):
    advance(scatter, 1)
    advance(gather, 1)
    advance(scatter, 8)
    advance(gather, 4)
    advance(scatter, 1)
    advance(gather)
    advance(scatter, 1)
    while advance(spread, 1):
        advance(scatter, 1)


def weave_ends(early, late, sends):
    advance(late, 5)
    advance(early, 1)
    advance(late, 4)
    for copy in sends:
        copy.wait_send()
    braid(early, late)


def layer_kernel(
    nodes, plan, x_ref, w_ref, cot_ref, tiles_ref, act_ref, wg_ref, fgt0, fgt1,
    tiles, staged, panel0, panel1, part0, part1, met0, met1, back0, back1,
    hid0, hid1, delta, cot, gt, met_rows, met_strips, strips, *rest
):
    f_bufs = (rest[0:6], rest[6:12])
    b_bufs = (rest[12:18], rest[18:24])
    mv = Mover(*rest[24:27])
    panel, part, met, back = (panel0, panel1), (part0, part1), (met0, met1), (back0, back1)
    hid, fgt = (hid0, hid1), (fgt0, fgt1)
    z, xh, xl, y, k = place()
    rows = cot.shape[0]
    blocks = rows // SIDE

    row_slot = lambda p, q: p * 2 + q
    col_slot = lambda p, q: (q * 4 + p) * 2 + k
    row_links = Links(
        (row_device((z + 1) % 4, xh), row_device((z + 3) % 4, xh)),
        row_device(z, 1 - xh), z, xh, row_slot, blocks)
    col_links = Links(
        (col_device(xl, (y + 1) % 4, k), col_device(xl, (y + 3) % 4, k)),
        col_device(1 - xl, y, k), y, xl, col_slot, blocks)
    twin = col_device(xl, y, 1 - k)

    loads = [
        mv.local(x_ref.at[:, :, pl.ds(h * SIDE, SIDE)], row_links.part(panel[h], 0, 0)) for h in (0, 1)
    ]
    count = tiles_ref.shape[0]
    load_tiles = mv.local(tiles_ref, tiles.at[pl.ds(0, count)])
    tiles[count] = jnp.zeros((SIDE, SIDE), BF16)
    load_cot = mv.local(cot_ref, cot)
    greet([*row_links.ring, row_links.pair, *col_links.ring, col_links.pair, twin])

    gathers = [gather_steps(mv, row_links, panel[h], GATHER_SHARE[h], lambda ref: None) for h in (0, 1)]
    loads[0].wait()
    advance(gathers[0], 7)
    loads[1].wait()
    advance(gathers[1], 1)
    advance(gathers[0])
    load_tiles.wait()

    def twin_steps(h):
        crossing = {}
        to_cross = list(ORDER)

        def cross(count):
            for d, side in to_cross[:count]:
                piece = (y + d) % 4 + 4 * (xl if side == 0 else 1 - xl)
                from_part = part[h].at[pl.ds((piece * 2 + 1 - k) * blocks, blocks)]
                to_met = met[h].at[pl.ds(piece * blocks, blocks)]
                crossing[d, side] = (mv.remote(from_part, to_met, twin), to_met)
            del to_cross[:count]

        cross(3)

        def ready(d, side):
            cross(1)
            copy, land = crossing[d, side]
            copy.wait_recv()
            ref = col_links.part(part[h], d, side)
            add_blocks(ref, [ref, land], blocks)

        yield from scatter_steps(mv, col_links, part[h], SCATTER_SHARE[h], f_bufs[h], hid[h], ready)

    cuts = 4
    spread = [
        spread_steps(plan, 0, False, tiles, panel[h], staged, part[h], cuts)
        for h in (0, 1)
    ]
    advance(spread[0], 2)
    advance(gathers[1], 1)
    advance(spread[0], 1)
    advance(gathers[1], 1)
    advance(spread[0])
    scatters = [twin_steps(h) for h in (0, 1)]
    weave(gathers[1], scatters[0], spread[1])
    forward_sends = mv.take()
    weave_ends(scatters[0], scatters[1], [])

    load_cot.wait()
    weight = w_ref[...]
    mine = col_links.piece(0, 0) * blocks

    def dense(i, carry):
        at = pl.ds(pl.multiple_of(i * SIDE, SIDE), SIDE)
        hidden = jnp.concatenate([hid0[i], hid1[i]], axis=1)
        pre = jnp.dot(hidden, weight, preferred_element_type=F32)
        sig = 1.0 / (1.0 + jnp.exp(-pre))
        act_ref[at, :] = (pre * sig).astype(BF16)
        d = (cot[at, :].astype(F32) * sig * (1.0 + pre * (1.0 - sig))).astype(BF16)
        delta[at, :] = d
        turned = lax.dot_general(
            weight, d, (((1,), (1,)), ((), ())), preferred_element_type=F32
        ).astype(BF16)
        for h in (0, 1):
            back[h][mine + i] = turned[h * SIDE:(h + 1) * SIDE]
        return carry

    lax.fori_loop(0, blocks, dense, 0)

    shares = [[], []]

    def arrived(h, ref):
        shares[h].append(mv.remote(ref, ref, twin))

    def gather_back(h):
        arrived(h, col_links.part(back[h], 0, 0))
        yield from gather_steps(mv, col_links, back[h], GATHER_SHARE[h], functools.partial(arrived, h))
        yield
        for share in shares[h]:
            share.wait_recv()

    gathers = [gather_back(h) for h in (0, 1)]
    advance(gathers[0], 1)
    for h in (0, 1):
        gt[h * SIDE:(h + 1) * SIDE, :] = lax.dot_general(
            hid[h][...].reshape(rows, SIDE), delta[...], (((0,), (0,)), ((), ())), preferred_element_type=F32
        )
    for copy in forward_sends:
        copy.wait_send()
    advance(gathers[0], 6)
    near = lambda i: i + 1 - 2 * (i % 2)
    halvings = (
        (twin, k),
        (col_links.pair, xl),
        (col_device(xl, near(y), k), (y + 1) // 2 % 2),
        (col_device(xl, 3 - y, k), y // 2),
    )
    doublings = (row_links.pair, row_device(near(z), xh), row_device(3 - z, xh))
    reduce = reduce_steps(mv, gt, met_rows, met_strips, strips, wg_ref, halvings, doublings, nodes)
    advance(reduce, 1)
    advance(gathers[1], 1)
    advance(gathers[0])
    spread = [
        spread_steps(plan, 1, True, tiles, back[h], staged, panel[h], cuts) for h in (0, 1)
    ]
    advance(spread[0], 2)
    advance(gathers[1], 1)
    advance(reduce, 1)
    advance(spread[0], 1)
    advance(gathers[1], 1)
    advance(reduce, 1)
    advance(spread[0])
    scatters = [
        scatter_steps(mv, row_links, panel[h], SCATTER_SHARE[h], b_bufs[h], fgt[h], lambda d, side: None) for h in (0, 1)
    ]
    weave(gathers[1], scatters[0], both(spread[1], reduce))
    backward_sends = mv.take()
    weave_ends(scatters[0], both(scatters[1], reduce), backward_sends)
    advance(reduce)

    mv.drain()


def layer(plan, features, weight, cotangent, values, nodes):
    rows, width = features.shape
    total, size, _ = values.shape
    n_row, n_col = lax.axis_size("row"), lax.axis_size("col")
    any_spec = pl.BlockSpec(memory_space=pl.ANY)
    vmem = pl.BlockSpec(memory_space=pltpu.VMEM)
    blocks = rows // SIDE
    half = lambda count: [pltpu.VMEM((count * blocks, SIDE, SIDE), BF16)] * 2
    return pl.pallas_call(
        functools.partial(layer_kernel, nodes),
        out_shape=(
            jax.ShapeDtypeStruct((rows, width), BF16),
            jax.ShapeDtypeStruct((width, width), F32),
            *[jax.ShapeDtypeStruct((blocks, SIDE, SIDE), BF16)] * 2,
        ),
        in_specs=[pl.BlockSpec(memory_space=pltpu.SMEM), any_spec, vmem, any_spec, any_spec],
        out_specs=(vmem,) * 4,
        scratch_shapes=[
            pltpu.VMEM((total + 1, size, size), BF16),
            pltpu.VMEM((pair_slots(total, n_col * blocks), size, size), BF16),
            *half(n_row),
            *half(n_col),
            *half(n_col // 2),
            *half(n_col),
            *half(1),
            pltpu.VMEM((rows, width), BF16),
            pltpu.VMEM((rows, width), BF16),
            pltpu.VMEM((width, width), F32),
            pltpu.VMEM((width, width), F32),
            pltpu.VMEM((3, width // n_col, width), F32),
            pltpu.VMEM((4, width // n_col, width), F32),
            *((scatter_scratch(blocks, SCATTER_SHARE[0]) + scatter_scratch(blocks, SCATTER_SHARE[1])) * 2),
            pltpu.SemaphoreType.DMA((280,)),
            pltpu.SemaphoreType.DMA((280,)),
            pltpu.SemaphoreType.DMA((4,)),
        ],
        compiler_params=pltpu.CompilerParams(
            collective_id=1, has_side_effects=True, vmem_limit_bytes=63 * 2**20
        ),
    )(plan, features.reshape(blocks, SIDE, width), weight, cotangent, values)


def unfold_kernel(act_ref, wg_ref, fgt0, fgt1, act_out, wg_out, fg_out):
    def body(i, carry):
        at = pl.ds(pl.multiple_of(i * SIDE, SIDE), SIDE)
        act_out[at, :] = act_ref[at, :]
        fg_out[at, :] = jnp.concatenate([fgt0[i].T, fgt1[i].T], axis=1)
        return carry

    lax.fori_loop(0, fgt0.shape[0], body, 0)
    wg_out[...] = wg_ref[...]


def unfold(activated, weight_grad, turned0, turned1):
    vmem = pl.BlockSpec(memory_space=pltpu.VMEM)
    like = lambda a: jax.ShapeDtypeStruct(a.shape, a.dtype)
    return pl.pallas_call(
        unfold_kernel,
        out_shape=(like(activated), like(weight_grad), like(activated)),
        in_specs=[vmem] * 4,
        out_specs=(vmem,) * 3,
    )(activated, weight_grad, turned0, turned1)


def pair_slots(total, blocks):
    need = (total + blocks) // 2
    return -(-need // UNROLL) * UNROLL


def paired_slots(dest, anchor, count, blocks, room):
    total = dest.shape[0]
    slot = jnp.arange(total, dtype=jnp.int32)
    block = jnp.arange(room, dtype=jnp.int32)
    add = lambda hit, value=1: jnp.sum(jnp.where(hit, value, 0), axis=1, dtype=jnp.int32)
    live = slot < count
    dest = jnp.where(live, dest, blocks)
    mine = add(dest[None, :] == block[:, None])
    pairs = (mine + 1) // 2
    start = add(block[None, :] < block[:, None], pairs[None, :])
    order = add((dest[None, :] == dest[:, None]) & (slot[None, :] < slot[:, None]))
    begin = add(dest[:, None] == block[None, :], start[None, :])
    at = jnp.where(live, begin + order // 2, room)
    here = at[None, :] == block[:, None]
    first = here & (order % 2 == 0)[None, :]
    second = here & (order % 2 == 1)[None, :]
    alone = 1 - add(second)
    tile0 = add(first, slot[None, :])
    tile1 = add(second, slot[None, :]) + alone * total
    anchor0 = add(first, anchor[None, :])
    anchor1 = add(second, anchor[None, :]) + alone * anchor0
    fresh = add(first & (order == 0)[None, :])
    return jnp.stack([tile0, tile1, anchor0, anchor1, fresh, jnp.maximum(start + pairs - 1, 0), mine])


def per_device(features, weight, cotangent, tile_values, tile_rows, tile_cols, tile_count):
    rows_idx = tile_rows[0, 0]
    cols_idx = tile_cols[0, 0]
    count = tile_count[0, 0]
    rows = features.shape[0]
    size = tile_values.shape[-1]
    n_row, n_col = lax.axis_size("row"), lax.axis_size("col")
    row_blocks, col_blocks = rows * n_col // size, rows * n_row // size
    room = pair_slots(rows_idx.shape[0], row_blocks)
    plan = jax.vmap(paired_slots, in_axes=(0, 0, None, 0, None))(
        jnp.stack([rows_idx, cols_idx]),
        jnp.stack([cols_idx, rows_idx]),
        count,
        jnp.array([row_blocks, col_blocks], jnp.int32),
        room,
    )
    return unfold(*layer(plan, features, weight, cotangent, tile_values[0, 0], rows * n_row * n_col))


def solution(mesh):
    return jax.shard_map(
        per_device,
        mesh=mesh,
        in_specs=(
            P(("col", "row"), None),
            P(),
            P(("row", "col"), None),
            P("row", "col", None, None, None),
            P("row", "col", None),
            P("row", "col", None),
            P("row", "col"),
        ),
        out_specs=(P(("row", "col"), None), P(), P(("col", "row"), None)),
        check_vma=False,
    )
```
